128 devices in a mesh: beam: 32 (over z, y, core), sub: 4 (over x).
Axes of the slice: x: 4, y: 4, z: 4, core: 2. Of those that a mesh axis runs over, the one named last changes fastest.
Arguments:
- voltages: bfloat16 [2, 32, 4, 798, 256], P(None, 'beam', 'sub'), may hold values from -6 to 6
- pfb_taps: float32 [16, 256], replicated, may hold values from -1.5 to 1.5
- delays: int32 [2048, 1024], replicated, may hold values from 0 to 15, as said below
- assignment: int32 [32, 32], replicated, may hold values from 0 to 31, each once within a row
- widths: int32 [8], replicated, may hold values from 1 to 32
Outputs:
- dm_series: bfloat16 [32, 32, 64, 768], P('beam', None, 'sub')
- snr: float32 [32, 32, 64, 8], P('beam', None, 'sub')
The draws below stay inside these ranges and needn't reach their ends.
Inputs may be any that keep to these rules, and one draw needn't show every extreme that they name: delays are nonnegative and below 16. Each row of assignment names every one of the 32 DM ranges once.
All inputs are finite; a program needn't handle non-finite values.
Results may differ from the reference program's by a relative error of at most 0.0048.
Values may be sent and summed in bfloat16 or wider, within the bound.
A program may use at most 128 MiB of HBM per device.

```python
import math
import jax
import jax.numpy as jnp
from jax import lax

FINE = 256
COARSE = 4
DMS = 2048
TAPS = 16
SHIFTS = 16
NBOX = 8
MAXW = 32
TOUT = 768
CHANS = 1024
BEAMS = 32
TINF = 798
N_BEAM = 32


def draw_delays(key, part):
    key = jax.random.fold_in(key, 7)
    measure_key = jax.random.fold_in(key, 1)
    offset_key = jax.random.fold_in(key, 2)
    jitter_key = jax.random.fold_in(key, 3)
    channels = COARSE * FINE
    measure = jax.random.randint(measure_key, (DMS, 1), 0, DMS, dtype=jnp.int32)
    offsets = jax.random.randint(offset_key, (1, channels), 0, SHIFTS // 2, dtype=jnp.int32)
    channel = jnp.arange(channels, dtype=jnp.int32)[None, :]
    reach = SHIFTS - 1 - offsets
    sweep = (channels - 1 - channel) * measure * reach // ((channels - 1) * (DMS - 1))
    jitter = jax.random.randint(jitter_key, (DMS, channels), -1, 2, dtype=jnp.int32)
    lookup = jnp.clip(offsets + sweep + jitter, 0, SHIFTS - 1)
    lookup = lookup.at[DMS - 1, 0].set(SHIFTS - 1)
    return lookup.at[0, channels - 1].set(0)


def draw_widths(key, part):
    key = jax.random.fold_in(key, 13)
    drawn = jax.random.randint(key, (NBOX,), 2, MAXW, dtype=jnp.int32)
    return drawn.at[0].set(1).at[NBOX - 1].set(MAXW)


def shard_levels(own_key, dims, shards, smallest, largest):
    def one(axis_at, blocks):
        draws = jax.random.uniform(jax.random.fold_in(jax.random.fold_in(own_key, 6), axis_at), (blocks,), jnp.float32, smallest / len(shards), largest / len(shards))
        return jnp.repeat(jnp.exp(draws), dims[axis_at] // blocks).reshape((-1,) + (1,) * (len(dims) - axis_at - 1))

    factor_of = one(*shards[0])
    for cut in shards[1:]:
        factor_of = factor_of * one(*cut)
    return factor_of


def centred(stream_key, dims, scale, most, shards=(), held_as=jnp.bfloat16):
    array = jax.random.normal(stream_key, dims, jnp.float32) * scale
    if len(shards) > 0:
        array = shard_levels(stream_key, dims, shards, -0.22, 0.18) * array
    return jnp.clip(array, min=-most, max=most).astype(held_as)


def setup_inputs(seed: int = 0) -> dict:
    seeds = jax.random.split(jax.random.key(seed), 6)
    voltages = centred(seeds[0], (2, BEAMS, COARSE, TINF, FINE), 1.0, 6.0, ((1, 32), (2, 4)))
    pfb_taps = centred(seeds[1], (TAPS, FINE), TAPS ** -0.5, 1.5, (), jnp.float32)
    delays = draw_delays(jax.random.fold_in(seeds[5], 71), 0)
    assignment = jax.vmap(lambda own: jax.random.permutation(own, N_BEAM))(jax.random.split(seeds[3], BEAMS)).reshape((BEAMS, BEAMS)).astype(jnp.int32)
    widths = draw_widths(jax.random.fold_in(seeds[5], 71), 0)
    return dict(voltages=voltages, pfb_taps=pfb_taps, delays=delays, assignment=assignment, widths=widths)


HIGHEST = lax.Precision.HIGHEST

def dft_table(fine_len):
    position = jnp.arange(fine_len, dtype=jnp.int32)
    phases = position[:, None] * position[None, :] % fine_len
    angles = phases.astype(jnp.float32) * (2.0 * math.pi / fine_len)
    cosine = jnp.cos(angles) / math.sqrt(fine_len)
    sine_part = jnp.sin(angles) / math.sqrt(fine_len)
    upper_half = jnp.concatenate([cosine, -sine_part], axis=1)
    lower_half = jnp.concatenate([sine_part, cosine], axis=1)
    return jnp.concatenate([upper_half, lower_half], axis=0)

def channelize(voltages, pfb_taps):
    frames = voltages.astype(jnp.float32)
    frames_out = frames.shape[-2] - pfb_taps.shape[0] + 1
    filtered = pfb_taps[0] * frames[..., 0:frames_out, :]
    for tap_index in range(1, pfb_taps.shape[0]):
        filtered = filtered + pfb_taps[tap_index] * frames[..., tap_index:tap_index + frames_out, :]
    fine_len = pfb_taps.shape[1]
    stacked = jnp.concatenate([filtered[0], filtered[1]], axis=-1)
    spectra = jnp.dot(stacked, dft_table(fine_len), precision=HIGHEST, preferred_element_type=jnp.float32)
    powers = spectra[..., :fine_len] ** 2 + spectra[..., fine_len:] ** 2
    return (powers - lax.optimization_barrier(jnp.mean(powers, axis=-2, keepdims=True))).astype(jnp.bfloat16)

def boxcar_table(widths, length):
    position = jnp.arange(length, dtype=jnp.int32)
    upper_ids = position[:, None, None]
    lower_ids = position[None, None, :]
    return (upper_ids >= lower_ids) & (upper_ids < lower_ids + widths[None, :, None])

def dedisperse(fine_power, delays):
    beam_count = fine_power.shape[0]
    blocking = 16
    levels = jnp.arange(SHIFTS, dtype=jnp.int32)

    def accumulate(accumulated, block_id):
        offset = block_id * blocking
        row_block = lax.dynamic_slice_in_dim(fine_power, offset, blocking, 1).astype(jnp.float32)
        hankel = jnp.stack([row_block[:, :, s:s + TOUT] for s in range(SHIFTS)], axis=2)
        hankel = jnp.transpose(hankel, (1, 2, 0, 3)).reshape(blocking * SHIFTS, beam_count * TOUT)
        lookup = lax.dynamic_slice_in_dim(delays, offset, blocking, 1)
        onehot = (lookup[:, :, None] == levels).astype(jnp.float32).reshape(DMS, blocking * SHIFTS)
        return (accumulated + jnp.dot(onehot, hankel, precision=HIGHEST, preferred_element_type=jnp.float32), None)
    start_sum = jnp.zeros((DMS, beam_count * TOUT), jnp.float32)
    accumulated, _ = lax.scan(accumulate, start_sum, jnp.arange(CHANS // blocking, dtype=jnp.int32))
    return jnp.transpose(accumulated.reshape(DMS, beam_count, TOUT), (1, 0, 2))

def reference(voltages, pfb_taps, delays, assignment, widths):
    fine_power = channelize(voltages, pfb_taps)
    beam_count = fine_power.shape[0]
    arranged = jnp.transpose(fine_power, (0, 1, 3, 2)).reshape(beam_count, CHANS, TOUT + SHIFTS - 1)
    accumulated = dedisperse(arranged, delays) * CHANS ** (-0.5)
    dm_span = DMS // N_BEAM
    row_ids = jnp.transpose(assignment)[:, :, None] * dm_span + jnp.arange(dm_span, dtype=jnp.int32)[None, None, :]
    anchor = jnp.arange(beam_count, dtype=jnp.int32)[None, :, None]
    dm_series = accumulated[anchor, row_ids].astype(jnp.bfloat16)
    flattened = dm_series.astype(jnp.float32).reshape(-1, TOUT)
    lookup = boxcar_table(widths, TOUT).astype(jnp.float32).reshape(TOUT, NBOX * TOUT)
    box_sums = jnp.dot(flattened, lookup, precision=HIGHEST, preferred_element_type=jnp.float32)
    best = lax.optimization_barrier(jnp.max(box_sums.reshape(-1, NBOX, TOUT), axis=-1)) / jnp.sqrt(widths.astype(jnp.float32))
    snr = best.reshape(beam_count, beam_count, dm_span, NBOX)
    return (dm_series, snr)
```

```python
import functools
import math

import jax
import jax.numpy as jnp
import numpy as np
from jax import lax
from jax.experimental import pallas as pl
from jax.experimental.pallas import tpu as pltpu
from jax.sharding import PartitionSpec as P

FINE = 256
COARSE = 4
TAPS = 16
SHIFTS = 16
NBOX = 8
MAXW = 32
TOUT = 768
FRAMES = TOUT + SHIFTS - 1
ROWS = 784
PIECE = 256
PIECES = TOUT // PIECE
CUTS = ((0, 272), (272, 256), (528, 256))
BLOCK = 112
MESH = pl.DeviceIdType.MESH
BF16 = jnp.bfloat16
F32 = jnp.float32


def dft_tables():
    position = np.arange(FINE)
    angles = (position[:, None] * position[None, :] % FINE) * (2.0 * math.pi / FINE)
    cosine = np.cos(angles) / math.sqrt(FINE)
    sine = np.sin(angles) / math.sqrt(FINE)
    table = np.concatenate(
        [np.concatenate([cosine, -sine], 1), np.concatenate([sine, cosine], 1)], 0
    ).astype(np.float32)
    high = table.astype(BF16)
    low = (table - high.astype(np.float32)).astype(BF16)
    return np.stack([high, low])


def channelize(volt_ref, taps_ref, table, frames, powers, own):
    frames[:, ROWS - 8 :, :] = jnp.zeros((2, frames.shape[1] - ROWS + 8, FINE), F32)
    for part in range(2):
        frames[part, 0 : volt_ref.shape[1], :] = volt_ref[part].astype(F32)
    taps = taps_ref[...]

    def step(index, total):
        start = pl.multiple_of(index * BLOCK, 16)
        halves = []
        for part in range(2):
            window = frames[part, pl.ds(start, BLOCK + TAPS), :]
            value = taps[0:1] * window[0:BLOCK]
            for tap in range(1, TAPS):
                value = value + taps[tap : tap + 1] * window[tap : tap + BLOCK]
            halves.append(value)
        stacked = jnp.concatenate(halves, axis=1)
        high = stacked.astype(BF16)
        low = (stacked - high.astype(F32)).astype(BF16)
        spectra = (
            jnp.dot(high, table[0], preferred_element_type=F32)
            + jnp.dot(low, table[0], preferred_element_type=F32)
            + jnp.dot(high, table[1], preferred_element_type=F32)
        )
        power = spectra[:, :FINE] ** 2 + spectra[:, FINE:] ** 2
        frame = start + lax.broadcasted_iota(jnp.int32, (BLOCK, FINE), 0)
        power = jnp.where(frame < FRAMES, power, 0.0)
        powers[pl.ds(start, BLOCK), :] = power
        return total + jnp.sum(power, axis=0, keepdims=True)

    total = lax.fori_loop(0, ROWS // BLOCK, step, jnp.zeros((1, FINE), F32))
    mean = total * (1.0 / FRAMES)

    @pl.loop(0, ROWS // BLOCK)
    def _(index):
        rows = pl.ds(pl.multiple_of(index * BLOCK, 16), BLOCK)
        own[0, rows, :] = (powers[rows, :] - mean).astype(BF16)


def search_kernel(
    beams,
    volt_ref,
    taps_ref,
    table_hbm,
    delays_hbm,
    assign_ref,
    out_ref,
    table,
    delays,
    frames,
    powers,
    slabs,
    onehot,
    shifted,
    total,
    outbox,
    load_sem,
    ring_send,
    ring_recv,
    block_send,
    block_recv,
    local_sem,
):
    me = lax.axis_index("beam")
    sub = lax.axis_index("sub")
    subs = COARSE
    left, right = lax.rem(sub + subs - 1, subs), lax.rem(sub + 1, subs)

    barrier = pltpu.get_barrier_semaphore()
    for side in (left, right):
        pl.semaphore_signal(barrier, inc=1, device_id={"sub": side}, device_id_type=MESH)

    @pl.loop(1, beams)
    def _(offset):
        peer = lax.rem(me + offset, beams)
        pl.semaphore_signal(barrier, inc=1, device_id={"beam": peer}, device_id_type=MESH)

    table_copy = pltpu.make_async_copy(table_hbm, table, load_sem.at[0])
    table_copy.start()
    delays_copy = pltpu.make_async_copy(
        delays_hbm.at[:, pl.ds(pl.multiple_of(sub * 16, 16), 16), :], delays, load_sem.at[1]
    )
    delays_copy.start()
    table_copy.wait()
    channelize(volt_ref, taps_ref, table, frames, powers, slabs)
    pl.semaphore_wait(barrier, 2 + beams - 1)

    def ring(source, target, first, count, side, which):
        return pltpu.make_async_remote_copy(
            src_ref=slabs.at[source, pl.ds(first, count)],
            dst_ref=slabs.at[target, pl.ds(first, count)],
            send_sem=ring_send.at[which],
            recv_sem=ring_recv.at[which],
            device_id={"sub": side},
            device_id_type=MESH,
        )

    near, far = [], []
    for piece, (first, count) in enumerate(CUTS):
        near.append(
            (
                ring(0, 1, first, count, right, 4 * piece),
                ring(0, 2, first, count, left, 4 * piece + 1),
            )
        )
        half = 128
        far.append(
            (
                ring(1, 3, first, half, right, 4 * piece + 2),
                ring(2, 3, first + half, count - half, left, 4 * piece + 3),
            )
        )

    def pass_on(piece):
        for arrived, onward in zip(near[piece], far[piece]):
            arrived.wait_recv()
            onward.start()

    for copy in near[0] + near[1]:
        copy.start()

    delays_copy.wait()

    @pl.loop(0, beams)
    def _(owner):
        rows = pl.ds(pl.multiple_of(owner * 16, 16), 16)
        for slot, hop in enumerate((0, subs - 1, 1, 2)):
            coarse = lax.rem(sub + hop, subs)
            lanes = pl.ds(pl.multiple_of(coarse * FINE, FINE), FINE)
            lookup = delays[assign_ref[me, owner], :, lanes].astype(F32).astype(BF16)
            for shift in range(SHIFTS):
                onehot[slot, rows, shift * FINE : (shift + 1) * FINE] = jnp.where(
                    lookup == BF16(shift), BF16(1), BF16(0)
                )

    def shift_rows(slot, piece):
        @pl.loop(0, PIECE // 32)
        def _(index):
            start = pl.multiple_of(index * 32, 32)
            window = slabs[slot, pl.ds(piece * PIECE + start, 48), :]
            for shift in range(SHIFTS):
                shifted[pl.ds(start, 32), shift * FINE : (shift + 1) * FINE] = window[
                    shift : shift + 32
                ]

    def add_slot(slot, piece, rows):
        product = lax.dot_general(
            onehot[slot, rows, :],
            shifted[...],
            (((1,), (1,)), ((), ())),
            preferred_element_type=F32,
        )
        if slot == 0:
            total[piece, rows, :] = product
        else:
            total[piece, rows, :] += product

    every = pl.ds(0, beams * 16)
    half_span = beams // 2
    scale = 1.0 / math.sqrt(COARSE * FINE)

    def block_copy(piece, owner):
        return pltpu.make_async_remote_copy(
            src_ref=outbox.at[piece, owner],
            dst_ref=out_ref.at[piece, me],
            send_sem=block_send.at[piece],
            recv_sem=block_recv.at[piece],
            device_id={"beam": owner},
            device_id_type=MESH,
        )

    def deliver(piece, part):
        rows = pl.ds(part * half_span * 16, half_span * 16)
        series = (total[piece, rows, :] * scale).astype(BF16)
        outbox[piece, pl.ds(part * half_span, half_span)] = series.reshape(
            half_span, 16, PIECE
        )

        @pl.loop(0, half_span)
        def _(offset):
            owner = part * half_span + lax.rem(me + offset, half_span)

            @pl.when(owner != me)
            def _():
                block_copy(piece, owner).start()

            @pl.when(owner == me)
            def _():
                pltpu.make_async_copy(
                    outbox.at[piece, me], out_ref.at[piece, me], local_sem.at[piece]
                ).start()

    for piece in range(PIECES):
        if piece == 1:
            pass_on(0)
            for copy in near[2]:
                copy.start()
        shift_rows(0, piece)
        add_slot(0, piece, every)
    pass_on(1)

    for piece in range(PIECES):
        for slot in (1, 2, 3):
            if piece == 0 and slot == 3:
                pass_on(2)
            if slot == 3:
                for copy in far[piece]:
                    copy.wait_recv()
            shift_rows(slot, piece)
            if slot < 3:
                add_slot(slot, piece, every)
            else:
                for part in range(2):
                    add_slot(slot, piece, pl.ds(part * half_span * 16, half_span * 16))
                    deliver(piece, part)

    for piece in range(PIECES):
        pltpu.make_async_copy(
            outbox.at[piece, me], out_ref.at[piece, me], local_sem.at[piece]
        ).wait()
        others = pltpu.make_async_remote_copy(
            src_ref=outbox.at[piece, pl.ds(0, beams - 1)],
            dst_ref=out_ref.at[piece, pl.ds(0, beams - 1)],
            send_sem=block_send.at[piece],
            recv_sem=block_recv.at[piece],
            device_id={"beam": me},
            device_id_type=MESH,
        )
        others.wait_recv()
        others.wait_send()
    for piece in range(PIECES):
        for copy in near[piece] + far[piece]:
            copy.wait_send()


def boxcar_kernel(widths_ref, blocks_ref, triangle_ref, series_ref, snr_ref, prefix):
    beams = blocks_ref.shape[1]
    rows = beams * 16
    for piece in range(PIECES):
        series_ref[0, :, :, piece * PIECE : (piece + 1) * PIECE] = blocks_ref[piece]
    series = series_ref[0].reshape(rows, TOUT)
    sums = lax.dot_general(
        triangle_ref[...], series, (((1,), (1,)), ((), ())), preferred_element_type=F32
    )
    lane_tiles = rows // 128
    for tile in range(lane_tiles):
        prefix[tile] = sums[:, tile * 128 : (tile + 1) * 128]
    for tile in range(lane_tiles):
        best = []
        for box in range(NBOX):
            width = widths_ref[box]

            def step(index, best_so_far):
                start = pl.multiple_of(index * 64, 64)
                window = prefix[tile, pl.ds(start + width, 64), :] - prefix[
                    tile, pl.ds(start, 64), :
                ]
                return jnp.maximum(best_so_far, jnp.max(window.reshape(8, 8, 128), axis=0))

            top = lax.fori_loop(0, TOUT // 64, step, jnp.full((8, 128), -jnp.inf, F32))
            top = jnp.max(top, axis=0, keepdims=True)
            best.append(top / jnp.sqrt(jnp.full((1, 128), width, jnp.int32).astype(F32)))
        best = jnp.concatenate(best, axis=0)
        snr_ref[0, pl.ds(tile * 8, 8), :, :] = best.T.reshape(8, 16, NBOX)


def on_device(beams, voltages, pfb_taps, delays, assignment, widths):
    span = delays.shape[0] // beams
    own_span = span // COARSE
    assert own_span == 16
    vmem = pl.BlockSpec(memory_space=pltpu.VMEM)
    smem = pl.BlockSpec(memory_space=pltpu.SMEM)
    anywhere = pl.BlockSpec(memory_space=pl.ANY)
    chans = COARSE * FINE
    rows = beams * own_span
    blocks = pl.pallas_call(
        functools.partial(search_kernel, beams),
        out_shape=jax.ShapeDtypeStruct((PIECES, beams, own_span, PIECE), BF16),
        in_specs=[vmem, vmem, anywhere, anywhere, smem],
        out_specs=anywhere,
        scratch_shapes=[
            pltpu.VMEM((2, 2 * FINE, 2 * FINE), BF16),
            pltpu.VMEM((beams, own_span, chans), jnp.int32),
            pltpu.VMEM((2, ROWS + 32, FINE), F32),
            pltpu.VMEM((ROWS, FINE), F32),
            pltpu.VMEM((COARSE, ROWS, FINE), BF16),
            pltpu.VMEM((COARSE, rows, SHIFTS * FINE), BF16),
            pltpu.VMEM((PIECE, SHIFTS * FINE), BF16),
            pltpu.VMEM((PIECES, rows, PIECE), F32),
            pltpu.VMEM((PIECES, beams, own_span, PIECE), BF16),
            pltpu.SemaphoreType.DMA((2,)),
            pltpu.SemaphoreType.DMA((4 * PIECES,)),
            pltpu.SemaphoreType.DMA((4 * PIECES,)),
            pltpu.SemaphoreType.DMA((PIECES,)),
            pltpu.SemaphoreType.DMA((PIECES,)),
            pltpu.SemaphoreType.DMA((PIECES,)),
        ],
        compiler_params=pltpu.CompilerParams(
            collective_id=0, has_side_effects=True, vmem_limit_bytes=56 << 20
        ),
    )(
        voltages.reshape(2, voltages.shape[-2], FINE),
        pfb_taps,
        jnp.asarray(dft_tables()),
        delays.reshape(beams, span, chans),
        assignment,
    )
    edge = np.arange(TOUT + MAXW)
    triangle = jnp.asarray((np.arange(TOUT)[None, :] < edge[:, None]).astype(BF16))
    return pl.pallas_call(
        boxcar_kernel,
        out_shape=(
            jax.ShapeDtypeStruct((1, beams, own_span, TOUT), BF16),
            jax.ShapeDtypeStruct((1, beams, own_span, NBOX), F32),
        ),
        in_specs=[smem, vmem, vmem],
        out_specs=(vmem, vmem),
        scratch_shapes=[pltpu.VMEM((rows // 128, TOUT + MAXW, 128), F32)],
        compiler_params=pltpu.CompilerParams(vmem_limit_bytes=32 << 20),
    )(widths, blocks, triangle)


def solution(mesh):
    in_specs = (P(None, "beam", "sub", None, None), P(), P(), P(), P())
    out_specs = (P("beam", None, "sub", None), P("beam", None, "sub", None))
    return jax.shard_map(
        functools.partial(on_device, mesh.shape["beam"]),
        mesh=mesh,
        in_specs=in_specs,
        out_specs=out_specs,
        check_vma=False,
    )
```

```python
import functools
import math

import jax
import jax.numpy as jnp
import numpy as np
from jax import lax
from jax.experimental import pallas as pl
from jax.experimental.pallas import tpu as pltpu
from jax.sharding import PartitionSpec as P

FINE = 256
COARSE = 4
TAPS = 16
SHIFTS = 16
NBOX = 8
MAXW = 32
TOUT = 768
FRAMES = TOUT + SHIFTS - 1
ROWS = 784
PIECE = 256
PIECES = TOUT // PIECE
CUTS = ((0, 272), (272, 256), (528, 256))
BLOCK = 392
MESH = pl.DeviceIdType.MESH
BF16 = jnp.bfloat16
F32 = jnp.float32


def dft_table():
    position = np.arange(FINE)
    angles = (position[:, None] * position[None, :] % FINE) * (2.0 * math.pi / FINE)
    cosine = np.cos(angles) / math.sqrt(FINE)
    sine = np.sin(angles) / math.sqrt(FINE)
    table = np.concatenate(
        [np.concatenate([cosine, -sine], 1), np.concatenate([sine, cosine], 1)], 0
    ).astype(np.float32)
    return table


def channelize(volt_ref, taps_ref, table, split, table_copy, frames, powers, own):
    count = volt_ref.shape[0]
    frames[count:, :] = jnp.zeros((frames.shape[0] - count, 128), F32)
    chunk = count // 7

    @pl.loop(0, 7)
    def _(index):
        rows = pl.ds(pl.multiple_of(index * chunk, 8), chunk)
        frames[rows, :] = volt_ref[rows, :].astype(F32)

    taps = taps_ref[...]
    table_copy.wait()
    table_high = table[...].astype(BF16)
    table_low = (table[...] - table_high.astype(F32)).astype(BF16)
    split[0] = table_high
    split[1] = table_low

    def step(index, total):
        start = pl.multiple_of(index * BLOCK, 8)
        halves = []
        for part in range(2):
            for side in range(2):
                weights = taps[:, side * 128 : (side + 1) * 128]
                value = 0.0
                for tap in range(TAPS):
                    first = 4 * (start + tap) + 2 * side + part
                    value = value + weights[tap : tap + 1] * frames[
                        pl.ds(first, BLOCK, stride=4), :
                    ]
                halves.append(value)
        stacked = jnp.concatenate(halves, axis=1)
        high = stacked.astype(BF16)
        low = (stacked - high.astype(F32)).astype(BF16)
        spectra = (
            jnp.dot(high, split[0], preferred_element_type=F32)
            + jnp.dot(low, split[0], preferred_element_type=F32)
            + jnp.dot(high, split[1], preferred_element_type=F32)
        )
        power = spectra[:, :FINE] ** 2 + spectra[:, FINE:] ** 2
        frame = start + lax.broadcasted_iota(jnp.int32, (BLOCK, FINE), 0)
        power = jnp.where(frame < FRAMES, power, 0.0)
        powers[pl.ds(start, BLOCK), :] = power
        return total + jnp.sum(power, axis=0, keepdims=True)

    total = lax.fori_loop(0, ROWS // BLOCK, step, jnp.zeros((1, FINE), F32))
    mean = total * (1.0 / FRAMES)

    @pl.loop(0, 7)
    def _(index):
        rows = pl.ds(pl.multiple_of(index * (ROWS // 7), 16), ROWS // 7)
        own[0, rows, :] = (powers[rows, :] - mean).astype(BF16)


def search_kernel(
    beams,
    volt_ref,
    taps_ref,
    table_hbm,
    delays_hbm,
    assign_ref,
    widths_ref,
    series_ref,
    snr_ref,
    table,
    split,
    delays,
    lookups,
    frames,
    powers,
    slabs,
    total,
    outbox,
    prefix,
    snr_out,
    snr_in,
    plane_sem,
    load_sem,
    ring_send,
    ring_recv,
    block_send,
    block_recv,
    local_sem,
    snr_send,
    snr_recv,
):
    me = lax.axis_index("beam")
    sub = lax.axis_index("sub")
    subs = COARSE
    left, right = lax.rem(sub + subs - 1, subs), lax.rem(sub + 1, subs)

    barrier = pltpu.get_barrier_semaphore()
    for side in (left, right):
        pl.semaphore_signal(barrier, inc=1, device_id={"sub": side}, device_id_type=MESH)

    line = 8
    planes = beams // line
    plane, place = lax.div(me, line), lax.rem(me, line)
    others_of_place = [
        lax.rem(plane + hop, planes) * line + place for hop in range(1, planes)
    ]
    others_of_plane = [
        plane * line + lax.rem(place + hop, line) for hop in range(1, line)
    ]
    hops = [(0, 0), (0, 1), (0, 3), (1, 0), (3, 0), (0, 2), (2, 0), (1, 1)]
    hops += [(3, 3), (1, 3), (3, 1), (1, 2), (2, 1), (3, 2), (2, 3), (2, 2)]
    hops = [hop for hop in reversed(hops) if hop[0] < planes]
    others = [
        lax.rem(plane + far, planes) * line
        + lax.rem(place + 2 * near, line)
        + (core if core == 0 else 1 - 2 * lax.rem(place, 2))
        for far, near in hops
        for core in range(2)
        if (far, near, core) != (0, 0, 0)
    ]
    for peer in others_of_place + others_of_plane:
        pl.semaphore_signal(barrier, inc=1, device_id={"beam": peer}, device_id_type=MESH)

    table_copy = pltpu.make_async_copy(table_hbm, table, load_sem.at[0])
    table_copy.start()
    delays_copy = pltpu.make_async_copy(
        delays_hbm.at[:, pl.ds(pl.multiple_of(sub * 16, 16), 16), :], delays, load_sem.at[1]
    )
    delays_copy.start()
    channelize(volt_ref, taps_ref, table, split, table_copy, frames, powers, slabs)
    pl.semaphore_wait(barrier, 2 + planes - 1 + line - 1)
    for peer in others_of_place:
        pl.semaphore_signal(plane_sem, inc=1, device_id={"beam": peer}, device_id_type=MESH)

    def ring(source, target, first, count, side, which):
        return pltpu.make_async_remote_copy(
            src_ref=slabs.at[source, pl.ds(first, count)],
            dst_ref=slabs.at[target, pl.ds(first, count)],
            send_sem=ring_send.at[which],
            recv_sem=ring_recv.at[which],
            device_id={"sub": side},
            device_id_type=MESH,
        )

    near, far = [], []
    for piece, (first, count) in enumerate(CUTS):
        near.append(
            (
                ring(0, 1, first, count, right, 4 * piece),
                ring(0, 2, first, count, left, 4 * piece + 1),
            )
        )
        half = 128
        far.append(
            (
                ring(1, 3, first, half, right, 4 * piece + 2),
                ring(2, 3, first + half, count - half, left, 4 * piece + 3),
            )
        )

    def pass_on(piece):
        for arrived, onward in zip(near[piece], far[piece]):
            arrived.wait_recv()
            onward.start()

    for copy in near[0]:
        copy.start()
    delays_copy.wait()

    @pl.loop(0, beams)
    def _(owner):
        rows = pl.ds(pl.multiple_of(owner * 16, 16), 16)
        for slot, hop in enumerate((0, subs - 1, 1, 2)):
            coarse = lax.rem(sub + hop, subs)
            lanes = pl.ds(pl.multiple_of(coarse * FINE, FINE), FINE)
            lookup = delays[assign_ref[me, owner], :, lanes]
            lookups[slot, rows, :] = lookup.astype(F32).astype(BF16)

    def product(slot, piece):
        start = pl.multiple_of(piece * PIECE, PIECE)
        window = slabs[slot, pl.ds(start, PIECE + SHIFTS), :]
        shifted = jnp.concatenate(
            [window[shift : shift + PIECE] for shift in range(SHIFTS)], axis=1
        )
        lookup = lookups[slot]
        onehot = jnp.concatenate(
            [jnp.where(lookup == BF16(shift), BF16(1), BF16(0)) for shift in range(SHIFTS)],
            axis=1,
        )
        return lax.dot_general(
            onehot, shifted, (((1,), (1,)), ((), ())), preferred_element_type=F32
        )

    scale = 1.0 / math.sqrt(COARSE * FINE)

    def columns(piece):
        return pl.ds(pl.multiple_of(piece * PIECE, PIECE), PIECE)

    def block_copy(piece, owner):
        return pltpu.make_async_remote_copy(
            src_ref=outbox.at[piece, owner],
            dst_ref=series_ref.at[0, me, :, columns(piece)],
            send_sem=block_send.at[piece],
            recv_sem=block_recv.at[piece],
            device_id={"beam": owner},
            device_id_type=MESH,
        )

    def own_copy(piece):
        return pltpu.make_async_copy(
            outbox.at[piece, me], series_ref.at[0, me, :, columns(piece)], local_sem.at[piece]
        )

    def deliver(piece):
        series = (total[piece] * scale).astype(BF16)
        outbox[piece] = series.reshape(beams, 16, PIECE)
        own_copy(piece).start()

        for owner in others:
            block_copy(piece, owner).start()

        count = PIECE + 16
        triangle = jnp.where(
            lax.broadcasted_iota(jnp.int32, (count, PIECE), 1)
            < lax.broadcasted_iota(jnp.int32, (count, PIECE), 0),
            1.0,
            0.0,
        ).astype(BF16)
        sums = lax.dot_general(
            triangle, series, (((1,), (1,)), ((), ())), preferred_element_type=F32
        )
        start = pl.multiple_of(piece * PIECE, PIECE)
        for tile in range(lane_tiles):
            carry = prefix[tile, pl.ds(start, 8), :][0:1]
            prefix[tile, pl.ds(start, count), :] = (
                sums[:, tile * 128 : (tile + 1) * 128] + carry
            )

    lane_tiles = beams * 16 // 128
    prefix[:, 0:8, :] = jnp.zeros((lane_tiles, 8, 128), F32)
    @pl.loop(0, PIECES)
    def _(piece):
        @pl.when(piece == 2)
        def _():
            for copy in near[1]:
                copy.start()

        total[piece] = product(0, piece)

    pass_on(0)

    @pl.loop(0, 3 * PIECES)
    def _(step):
        piece = lax.div(step, 3)
        slot = 1 + lax.rem(step, 3)

        @pl.when(step == 2)
        def _():
            for copy in near[2]:
                copy.start()
            pl.semaphore_wait(plane_sem, planes - 1)

        for later in range(1, PIECES):

            @pl.when(step == 3 * later)
            def _():
                pass_on(later)

        for now in range(PIECES):

            @pl.when(step == 3 * now + 2)
            def _():
                for copy in far[now]:
                    copy.wait_recv()

        total[piece] += product(slot, piece)

        @pl.when(slot == 3)
        def _():
            deliver(piece)

    boxcars(widths_ref, prefix, snr_out)
    snr_in[pl.ds(me, 1)] = snr_out[pl.ds(me, 1)]

    for owner in others:
        pltpu.make_async_remote_copy(
            src_ref=snr_out.at[owner],
            dst_ref=snr_in.at[me],
            send_sem=snr_send,
            recv_sem=snr_recv,
            device_id={"beam": owner},
            device_id_type=MESH,
        ).start()

    for piece in range(PIECES):
        own_copy(piece).wait()
        all_blocks = pltpu.make_async_remote_copy(
            src_ref=outbox.at[piece, pl.ds(0, beams - 1)],
            dst_ref=series_ref.at[0, pl.ds(0, beams - 1), :, columns(piece)],
            send_sem=block_send.at[piece],
            recv_sem=block_recv.at[piece],
            device_id={"beam": me},
            device_id_type=MESH,
        )
        all_blocks.wait_recv()
        all_blocks.wait_send()
    all_snr = pltpu.make_async_remote_copy(
        src_ref=snr_out.at[pl.ds(0, beams - 1)],
        dst_ref=snr_in.at[pl.ds(0, beams - 1)],
        send_sem=snr_send,
        recv_sem=snr_recv,
        device_id={"beam": me},
        device_id_type=MESH,
    )
    all_snr.wait_recv()
    all_snr.wait_send()
    for piece in range(PIECES):
        for copy in near[piece] + far[piece]:
            copy.wait_send()
    snr_ref[...] = jnp.transpose(snr_in[:, :, 0:16], (2, 1, 0))


def boxcars(widths_ref, prefix, snr_out):
    lane_tiles = prefix.shape[0]
    block = 64
    widths = [widths_ref[box] for box in range(NBOX)]
    root = [
        1.0 / jnp.sqrt(jnp.full((1, 128), width, jnp.int32).astype(F32)) for width in widths
    ]
    tail = prefix.shape[1] - TOUT
    for tile in range(lane_tiles):
        prefix[tile, TOUT:, :] = jnp.broadcast_to(
            prefix[tile, TOUT : TOUT + 8, :][0:1], (tail, 128)
        )

    @pl.loop(0, lane_tiles)
    def _(tile):
        def step(index, best):
            start = pl.multiple_of(index * block, block)
            base = prefix[tile, pl.ds(start, block), :]
            out = []
            for box in range(NBOX):
                gain = prefix[tile, pl.ds(start + widths[box], block), :] - base
                top = jnp.max(gain.reshape(block // 8, 8, 128), axis=0)
                out.append(jnp.maximum(best[box], top))
            return tuple(out)

        best = lax.fori_loop(
            0, TOUT // block, step, tuple(jnp.full((8, 128), -jnp.inf, F32) for _ in range(NBOX))
        )
        best = jnp.concatenate(
            [jnp.max(top, axis=0, keepdims=True) * root[box] for box, top in enumerate(best)],
            axis=0,
        )
        for owner in range(8):
            snr_out[tile * 8 + owner] = pltpu.roll(best, (128 - 16 * owner) % 128, 1)


def on_device(beams, voltages, pfb_taps, delays, assignment, widths):
    span = delays.shape[0] // beams
    own_span = span // COARSE
    assert own_span == 16
    vmem = pl.BlockSpec(memory_space=pltpu.VMEM)
    smem = pl.BlockSpec(memory_space=pltpu.SMEM)
    anywhere = pl.BlockSpec(memory_space=pl.ANY)
    chans = COARSE * FINE
    rows = beams * own_span
    series, snr = pl.pallas_call(
        functools.partial(search_kernel, beams),
        out_shape=(
            jax.ShapeDtypeStruct((1, beams, own_span, TOUT), BF16),
            jax.ShapeDtypeStruct((own_span, NBOX, beams), F32),
        ),
        in_specs=[vmem, vmem, anywhere, anywhere, smem, smem],
        out_specs=(anywhere, vmem),
        scratch_shapes=[
            pltpu.VMEM((2 * FINE, 2 * FINE), F32),
            pltpu.VMEM((2, 2 * FINE, 2 * FINE), BF16),
            pltpu.VMEM((beams, own_span, chans), jnp.int32),
            pltpu.VMEM((COARSE, rows, FINE), BF16),
            pltpu.VMEM((4 * (ROWS + 16), 128), F32),
            pltpu.VMEM((ROWS, FINE), F32),
            pltpu.VMEM((COARSE, ROWS, FINE), BF16),
            pltpu.VMEM((PIECES, rows, PIECE), F32),
            pltpu.VMEM((PIECES, beams, own_span, PIECE), BF16),
            pltpu.VMEM((rows // 128, TOUT + MAXW + 8, 128), F32),
            pltpu.VMEM((beams, NBOX, 128), F32),
            pltpu.VMEM((beams, NBOX, 128), F32),
            pltpu.SemaphoreType.REGULAR,
            pltpu.SemaphoreType.DMA((2,)),
            pltpu.SemaphoreType.DMA((4 * PIECES,)),
            pltpu.SemaphoreType.DMA((4 * PIECES,)),
            pltpu.SemaphoreType.DMA((PIECES,)),
            pltpu.SemaphoreType.DMA((PIECES,)),
            pltpu.SemaphoreType.DMA((PIECES,)),
            pltpu.SemaphoreType.DMA,
            pltpu.SemaphoreType.DMA,
        ],
        compiler_params=pltpu.CompilerParams(
            collective_id=0, has_side_effects=True, vmem_limit_bytes=60 << 20
        ),
    )(
        voltages.reshape(2, -1, 2, 128).transpose(1, 2, 0, 3).reshape(-1, 128),
        pfb_taps,
        jnp.asarray(dft_table()),
        delays.reshape(beams, span, chans),
        assignment,
        widths,
    )
    return series, snr.transpose(2, 0, 1)[None]


def solution(mesh):
    in_specs = (P(None, "beam", "sub", None, None), P(), P(), P(), P())
    out_specs = (P("beam", None, "sub", None), P("beam", None, "sub", None))
    return jax.shard_map(
        functools.partial(on_device, mesh.shape["beam"]),
        mesh=mesh,
        in_specs=in_specs,
        out_specs=out_specs,
        check_vma=False,
    )
```

```python
import functools
import math

import jax
import jax.numpy as jnp
import numpy as np
from jax import lax
from jax.experimental import pallas as pl
from jax.experimental.pallas import tpu as pltpu
from jax.sharding import PartitionSpec as P

FINE = 256
COARSE = 4
TAPS = 16
SHIFTS = 16
NBOX = 8
MAXW = 32
TOUT = 768
FRAMES = TOUT + SHIFTS - 1
ROWS = 784
PIECE = 256
PIECES = TOUT // PIECE
CUTS = ((0, 272), (272, 256), (528, 256))
BLOCK = 392
MESH = pl.DeviceIdType.MESH
BF16 = jnp.bfloat16
F32 = jnp.float32


def dft_table():
    position = np.arange(FINE)
    angles = (position[:, None] * position[None, :] % FINE) * (2.0 * math.pi / FINE)
    return (np.stack([np.cos(angles), np.sin(angles)]) / math.sqrt(FINE)).astype(np.float32)


def channelize(
    volt_hbm, taps_ref, volt, volt_copies, table, split, table_copy, start_late, frames, powers, own
):
    count = volt_hbm.shape[0]
    frames[count:, :] = jnp.zeros((frames.shape[0] - count, 128), F32)
    for copy, rows in volt_copies:
        copy.wait()
        frames[rows, :] = volt[rows, :].astype(F32)
    table_copy.wait()
    for index in range(2):
        exact = table[index]
        high = exact.astype(BF16)
        low = (exact - high.astype(F32)).astype(BF16)
        for which, value in enumerate((high, low)):
            if index == 0:
                split[which, 0:FINE, 0:FINE] = value
                split[which, FINE:, FINE:] = value
            else:
                split[which, 0:FINE, FINE:] = -value
                split[which, FINE:, 0:FINE] = value
    start_late()
    taps = taps_ref[...]

    def step(index, total):
        start = pl.multiple_of(index * BLOCK, 8)
        halves = []
        for part in range(2):
            for side in range(2):
                weights = taps[:, side * 128 : (side + 1) * 128]
                value = 0.0
                for tap in range(TAPS):
                    first = 4 * (start + tap) + 2 * side + part
                    value = value + weights[tap : tap + 1] * frames[
                        pl.ds(first, BLOCK, stride=4), :
                    ]
                halves.append(value)
        stacked = jnp.concatenate(halves, axis=1)
        high = stacked.astype(BF16)
        low = (stacked - high.astype(F32)).astype(BF16)
        spectra = (
            jnp.dot(high, split[0], preferred_element_type=F32)
            + jnp.dot(low, split[0], preferred_element_type=F32)
            + jnp.dot(high, split[1], preferred_element_type=F32)
        )
        power = spectra[:, :FINE] ** 2 + spectra[:, FINE:] ** 2
        frame = start + lax.broadcasted_iota(jnp.int32, (BLOCK, FINE), 0)
        power = jnp.where(frame < FRAMES, power, 0.0)
        powers[pl.ds(start, BLOCK), :] = power
        return total + jnp.sum(power, axis=0, keepdims=True)

    total = lax.fori_loop(0, ROWS // BLOCK, step, jnp.zeros((1, FINE), F32))
    mean = total * (1.0 / FRAMES)

    @pl.loop(0, 7)
    def _(index):
        rows = pl.ds(pl.multiple_of(index * (ROWS // 7), 16), ROWS // 7)
        own[0, rows, :] = (powers[rows, :] - mean).astype(BF16)


def search_kernel(
    beams,
    volt_hbm,
    taps_ref,
    table_hbm,
    delays_hbm,
    assign_ref,
    widths_ref,
    series_ref,
    snr_ref,
    volt,
    table,
    split,
    delays,
    lookups,
    frames,
    powers,
    slabs,
    total,
    outbox,
    inbox,
    prefix,
    best,
    snr_out,
    plane_sem,
    volt_sem,
    load_sem,
    ring_send,
    ring_recv,
    block_send,
    block_recv,
    local_sem,
):
    me = lax.axis_index("beam")
    sub = lax.axis_index("sub")
    subs = COARSE
    left, right = lax.rem(sub + subs - 1, subs), lax.rem(sub + 1, subs)

    volt_copies = []
    for half in range(2):
        rows = pl.ds(half * (volt.shape[0] // 2), volt.shape[0] // 2)
        copy = pltpu.make_async_copy(volt_hbm.at[rows], volt.at[rows], volt_sem.at[half])
        copy.start()
        volt_copies.append((copy, rows))
    table_copy = pltpu.make_async_copy(table_hbm, table, load_sem.at[0])
    table_copy.start()

    barrier = pltpu.get_barrier_semaphore()
    for side in (left, right):
        pl.semaphore_signal(barrier, inc=1, device_id={"sub": side}, device_id_type=MESH)

    line = 8
    planes = beams // line
    plane, place = lax.div(me, line), lax.rem(me, line)
    others_of_place = [
        lax.rem(plane + hop, planes) * line + place for hop in range(1, planes)
    ]
    others_of_plane = [
        plane * line + lax.rem(place + hop, line) for hop in range(1, line)
    ]
    hops = [(0, 0), (0, 1), (0, 3), (1, 0), (3, 0), (0, 2), (2, 0), (1, 1)]
    hops += [(3, 3), (1, 3), (3, 1), (1, 2), (2, 1), (3, 2), (2, 3), (2, 2)]
    hops = [hop for hop in reversed(hops) if hop[0] < planes]
    others = [
        lax.rem(plane + far, planes) * line
        + lax.rem(place + 2 * near, line)
        + (core if core == 0 else 1 - 2 * lax.rem(place, 2))
        for far, near in hops
        for core in range(2)
        if (far, near, core) != (0, 0, 0)
    ]
    for peer in others_of_place + others_of_plane:
        pl.semaphore_signal(barrier, inc=1, device_id={"beam": peer}, device_id_type=MESH)

    delays_copy = pltpu.make_async_copy(
        delays_hbm.at[:, pl.ds(pl.multiple_of(sub * 16, 16), 16), :], delays, load_sem.at[1]
    )
    channelize(
        volt_hbm,
        taps_ref,
        volt,
        volt_copies,
        table,
        split,
        table_copy,
        delays_copy.start,
        frames,
        powers,
        slabs,
    )
    pl.semaphore_wait(barrier, 2 + planes - 1 + line - 1)
    for peer in others_of_place:
        pl.semaphore_signal(plane_sem, inc=1, device_id={"beam": peer}, device_id_type=MESH)

    def ring(source, target, first, count, side, which):
        return pltpu.make_async_remote_copy(
            src_ref=slabs.at[source, pl.ds(first, count)],
            dst_ref=slabs.at[target, pl.ds(first, count)],
            send_sem=ring_send.at[which],
            recv_sem=ring_recv.at[which],
            device_id={"sub": side},
            device_id_type=MESH,
        )

    near, far = [], []
    for piece, (first, count) in enumerate(CUTS):
        near.append(
            (
                ring(0, 1, first, count, right, 4 * piece),
                ring(0, 2, first, count, left, 4 * piece + 1),
            )
        )
        half = 128
        far.append(
            (
                ring(1, 3, first, half, right, 4 * piece + 2),
                ring(2, 3, first + half, count - half, left, 4 * piece + 3),
            )
        )

    def pass_on(piece):
        for arrived, onward in zip(near[piece], far[piece]):
            arrived.wait_recv()
            onward.start()

    for copy in near[0]:
        copy.start()
    delays_copy.wait()

    @pl.loop(0, beams)
    def _(owner):
        rows = pl.ds(pl.multiple_of(owner * 16, 16), 16)
        for slot, hop in enumerate((0, subs - 1, 1, 2)):
            coarse = lax.rem(sub + hop, subs)
            lanes = pl.ds(pl.multiple_of(coarse * FINE, FINE), FINE)
            lookup = delays[assign_ref[me, owner], :, lanes]
            lookups[slot, rows, :] = lookup.astype(F32).astype(BF16)

    def product(slots, start, count):
        onehots, shifts = [], []
        for slot in slots:
            window = slabs[slot, pl.ds(start, count + SHIFTS), :]
            lookup = lookups[slot]
            for shift in range(SHIFTS):
                shifts.append(window[shift : shift + count])
                onehots.append(jnp.where(lookup == BF16(shift), BF16(1), BF16(0)))
        return lax.dot_general(
            jnp.concatenate(onehots, axis=1),
            jnp.concatenate(shifts, axis=1),
            (((1,), (1,)), ((), ())),
            preferred_element_type=F32,
        )

    scale = 1.0 / math.sqrt(COARSE * FINE)

    def columns(piece):
        return pl.ds(pl.multiple_of(piece * PIECE, PIECE), PIECE)

    def block_copy(piece, owner):
        return pltpu.make_async_remote_copy(
            src_ref=outbox.at[piece, owner],
            dst_ref=inbox.at[piece, me],
            send_sem=block_send.at[piece],
            recv_sem=block_recv.at[piece],
            device_id={"beam": owner},
            device_id_type=MESH,
        )

    def out_copy(piece):
        return pltpu.make_async_copy(
            inbox.at[piece], series_ref.at[0, :, :, columns(piece)], local_sem.at[piece]
        )

    def deliver(piece):
        series = (total[piece] * scale).astype(BF16)
        outbox[piece] = series.reshape(beams, 16, PIECE)
        for owner in others:
            block_copy(piece, owner).start()
        inbox[piece, pl.ds(me, 1)] = outbox[piece, pl.ds(me, 1)]

    def add_prefix(piece, series):
        count = PIECE + MAXW + 16
        triangle = jnp.where(
            lax.broadcasted_iota(jnp.int32, (count, PIECE), 1)
            < lax.broadcasted_iota(jnp.int32, (count, PIECE), 0),
            1.0,
            0.0,
        ).astype(BF16)
        sums = lax.dot_general(
            triangle, series, (((1,), (1,)), ((), ())), preferred_element_type=F32
        )
        start = pl.multiple_of(piece * PIECE, PIECE)
        for tile in range(lane_tiles):
            carry = prefix[tile, pl.ds(start, 8), :][0:1]
            prefix[tile, pl.ds(start, count), :] = (
                sums[:, tile * 128 : (tile + 1) * 128] + carry
            )

    lane_tiles = beams * 16 // 128
    prefix[:, 0:8, :] = jnp.zeros((lane_tiles, 8, 128), F32)
    best[...] = jnp.full(best.shape, -jnp.inf, F32)
    widths = [widths_ref[box] for box in range(NBOX)]
    own = product((0,), 0, TOUT)
    for piece in range(PIECES):
        total[piece] = own[:, piece * PIECE : (piece + 1) * PIECE]
    pass_on(0)
    for copy in near[1]:
        copy.start()

    @pl.loop(0, PIECES)
    def _(piece):
        start = pl.multiple_of(piece * PIECE, PIECE)
        for later in range(1, PIECES):

            @pl.when(piece == later)
            def _():
                pass_on(later)

        @pl.loop(1, 3)
        def _(slot):
            total[piece] += product((slot,), start, PIECE)


        @pl.when(piece == 0)
        def _():
            for copy in near[2]:
                copy.start()
            pl.semaphore_wait(plane_sem, planes - 1)

        for now in range(PIECES):

            @pl.when(piece == now)
            def _():
                for copy in far[now]:
                    copy.wait_recv()

        total[piece] += product((3,), start, PIECE)

        deliver(piece)

    @pl.loop(0, PIECES)
    def _(piece):
        all_blocks = pltpu.make_async_remote_copy(
            src_ref=outbox.at[piece, pl.ds(0, beams - 1)],
            dst_ref=inbox.at[piece, pl.ds(0, beams - 1)],
            send_sem=block_send.at[piece],
            recv_sem=block_recv.at[piece],
            device_id={"beam": me},
            device_id_type=MESH,
        )
        all_blocks.wait_recv()
        out_copy(piece).start()
        add_prefix(piece, inbox[piece].reshape(beams * 16, PIECE))
        first = jnp.where(piece == 0, 0, piece * PIECE - MAXW)
        stop = jnp.where(piece == PIECES - 1, TOUT, (piece + 1) * PIECE - MAXW)
        boxcars(widths, prefix, best, first, stop)
        all_blocks.wait_send()

    finish_boxcars(widths, best, snr_out)
    snr_ref[...] = jnp.transpose(snr_out[:, :, 0:16], (2, 1, 0))
    for piece in range(PIECES):
        out_copy(piece).wait()
    for piece in range(PIECES):
        for copy in near[piece] + far[piece]:
            copy.wait_send()


def boxcars(widths, prefix, best, first, stop):
    block = MAXW

    @pl.loop(0, prefix.shape[0])
    def _(tile):
        def step(index, tops):
            start = pl.multiple_of(first + index * block, block)
            base = prefix[tile, pl.ds(start, block), :]
            out = []
            for box in range(NBOX):
                gain = prefix[tile, pl.ds(start + widths[box], block), :] - base
                top = jnp.max(gain.reshape(block // 8, 8, 128), axis=0)
                out.append(jnp.maximum(tops[box], top))
            return tuple(out)

        tops = tuple(best[tile, box] for box in range(NBOX))
        tops = lax.fori_loop(0, (stop - first) // block, step, tops)
        for box in range(NBOX):
            best[tile, box] = tops[box]


def finish_boxcars(widths, best, snr_out):
    root = [
        1.0 / jnp.sqrt(jnp.full((1, 128), width, jnp.int32).astype(F32)) for width in widths
    ]

    @pl.loop(0, best.shape[0])
    def _(tile):
        rows = [
            jnp.max(best[tile, box], axis=0, keepdims=True) * root[box] for box in range(NBOX)
        ]
        rows = jnp.concatenate(rows, axis=0)
        for owner in range(8):
            snr_out[tile * 8 + owner] = pltpu.roll(rows, (128 - 16 * owner) % 128, 1)


def hand_over(chunks, series_from, snr_from, series_to, snr_to, series, snr, into, out):
    count = series.shape[1] // chunks
    steps = [(snr_from, snr, snr_to)]
    for chunk in range(chunks):
        rows = pl.ds(chunk * count, count)
        steps.append((series_from.at[:, rows], series.at[:, rows], series_to.at[:, rows]))
    loads = [
        pltpu.make_async_copy(source, held, into.at[index])
        for index, (source, held, target) in enumerate(steps)
    ]
    stores = [
        pltpu.make_async_copy(held, target, out.at[index])
        for index, (source, held, target) in enumerate(steps)
    ]
    for load in loads:
        load.start()
    for load, store in zip(loads, stores):
        load.wait()
        store.start()
    for store in stores:
        store.wait()


def on_device(beams, voltages, pfb_taps, delays, assignment, widths):
    span = delays.shape[0] // beams
    own_span = span // COARSE
    assert own_span == 16
    vmem = pl.BlockSpec(memory_space=pltpu.VMEM)
    smem = pl.BlockSpec(memory_space=pltpu.SMEM)
    anywhere = pl.BlockSpec(memory_space=pl.ANY)
    chans = COARSE * FINE
    rows = beams * own_span
    series, snr = pl.pallas_call(
        functools.partial(search_kernel, beams),
        out_shape=(
            jax.ShapeDtypeStruct((1, beams, own_span, TOUT), BF16),
            jax.ShapeDtypeStruct((own_span, NBOX, beams), F32),
        ),
        in_specs=[anywhere, vmem, anywhere, anywhere, smem, smem],
        out_specs=(anywhere, vmem),
        scratch_shapes=[
            pltpu.VMEM((4 * voltages.shape[-2], 128), BF16),
            pltpu.VMEM((2, FINE, FINE), F32),
            pltpu.VMEM((2, 2 * FINE, 2 * FINE), BF16),
            pltpu.VMEM((beams, own_span, chans), jnp.int32),
            pltpu.VMEM((COARSE, rows, FINE), BF16),
            pltpu.VMEM((4 * (ROWS + 16), 128), F32),
            pltpu.VMEM((ROWS, FINE), F32),
            pltpu.VMEM((COARSE, ROWS, FINE), BF16),
            pltpu.VMEM((PIECES, rows, PIECE), F32),
            pltpu.VMEM((PIECES, beams, own_span, PIECE), BF16),
            pltpu.VMEM((PIECES, beams, own_span, PIECE), BF16),
            pltpu.VMEM((rows // 128, TOUT + MAXW + 16, 128), F32),
            pltpu.VMEM((rows // 128, NBOX, 8, 128), F32),
            pltpu.VMEM((beams, NBOX, 128), F32),
            pltpu.SemaphoreType.REGULAR,
            pltpu.SemaphoreType.DMA((2,)),
            pltpu.SemaphoreType.DMA((2,)),
            pltpu.SemaphoreType.DMA((4 * PIECES,)),
            pltpu.SemaphoreType.DMA((4 * PIECES,)),
            pltpu.SemaphoreType.DMA((PIECES,)),
            pltpu.SemaphoreType.DMA((PIECES,)),
            pltpu.SemaphoreType.DMA((PIECES,)),
        ],
        compiler_params=pltpu.CompilerParams(
            collective_id=0, has_side_effects=True, vmem_limit_bytes=60 << 20
        ),
    )(
        voltages.reshape(2, -1, 2, 128).transpose(1, 2, 0, 3).reshape(-1, 128),
        pfb_taps,
        jnp.asarray(dft_table()),
        delays.reshape(beams, span, chans),
        assignment,
        widths,
    )
    chunks = 8
    series, snr = pl.pallas_call(
        functools.partial(hand_over, chunks),
        out_shape=(
            jax.ShapeDtypeStruct(series.shape, series.dtype),
            jax.ShapeDtypeStruct(snr.shape, snr.dtype),
        ),
        in_specs=[anywhere, anywhere],
        out_specs=(anywhere, anywhere),
        scratch_shapes=[
            pltpu.VMEM(series.shape, series.dtype),
            pltpu.VMEM(snr.shape, snr.dtype),
            pltpu.SemaphoreType.DMA((chunks + 1,)),
            pltpu.SemaphoreType.DMA((chunks + 1,)),
        ],
        compiler_params=pltpu.CompilerParams(vmem_limit_bytes=60 << 20),
    )(series, snr)
    return series, snr.transpose(2, 0, 1)[None]


def solution(mesh):
    in_specs = (P(None, "beam", "sub", None, None), P(), P(), P(), P())
    out_specs = (P("beam", None, "sub", None), P("beam", None, "sub", None))
    return jax.shard_map(
        functools.partial(on_device, mesh.shape["beam"]),
        mesh=mesh,
        in_specs=in_specs,
        out_specs=out_specs,
        check_vma=False,
    )
```

```python
import functools
import math

import jax
import jax.numpy as jnp
import numpy as np
from jax import lax
from jax.experimental import pallas as pl
from jax.experimental.pallas import tpu as pltpu
from jax.sharding import PartitionSpec as P

FINE = 256
COARSE = 4
TAPS = 16
SHIFTS = 16
NBOX = 8
MAXW = 32
TOUT = 768
FRAMES = TOUT + SHIFTS - 1
ROWS = 784
PIECE = 256
PIECES = TOUT // PIECE
CUTS = ((0, 272), (272, 256), (528, 256))
BLOCK = 392
MESH = pl.DeviceIdType.MESH
BF16 = jnp.bfloat16
F32 = jnp.float32


def dft_table():
    position = np.arange(FINE)
    angles = (position[:, None] * position[None, :] % FINE) * (2.0 * math.pi / FINE)
    return (np.stack([np.cos(angles), np.sin(angles)]) / math.sqrt(FINE)).astype(np.float32)


def channelize(
    volt_hbm, taps_ref, volt, volt_copies, table, split, table_copy, start_late, frames, powers, own
):
    count = volt_hbm.shape[0]
    frames[count:, :] = jnp.zeros((frames.shape[0] - count, 128), F32)
    for copy, rows in volt_copies:
        copy.wait()
        frames[rows, :] = volt[rows, :].astype(F32)
    table_copy.wait()
    for index in range(2):
        exact = table[index]
        high = exact.astype(BF16)
        low = (exact - high.astype(F32)).astype(BF16)
        for which, value in enumerate((high, low)):
            if index == 0:
                split[which, 0:FINE, 0:FINE] = value
                split[which, FINE:, FINE:] = value
            else:
                split[which, 0:FINE, FINE:] = -value
                split[which, FINE:, 0:FINE] = value
    start_late()
    taps = taps_ref[...]

    def step(index, total):
        start = pl.multiple_of(index * BLOCK, 8)
        halves = []
        for part in range(2):
            for side in range(2):
                weights = taps[:, side * 128 : (side + 1) * 128]
                value = 0.0
                for tap in range(TAPS):
                    first = 4 * (start + tap) + 2 * side + part
                    value = value + weights[tap : tap + 1] * frames[
                        pl.ds(first, BLOCK, stride=4), :
                    ]
                halves.append(value)
        stacked = jnp.concatenate(halves, axis=1)
        high = stacked.astype(BF16)
        low = (stacked - high.astype(F32)).astype(BF16)
        spectra = (
            jnp.dot(high, split[0], preferred_element_type=F32)
            + jnp.dot(low, split[0], preferred_element_type=F32)
            + jnp.dot(high, split[1], preferred_element_type=F32)
        )
        power = spectra[:, :FINE] ** 2 + spectra[:, FINE:] ** 2
        frame = start + lax.broadcasted_iota(jnp.int32, (BLOCK, FINE), 0)
        power = jnp.where(frame < FRAMES, power, 0.0)
        powers[pl.ds(start, BLOCK), :] = power
        return total + jnp.sum(power, axis=0, keepdims=True)

    total = lax.fori_loop(0, ROWS // BLOCK, step, jnp.zeros((1, FINE), F32))
    mean = total * (1.0 / FRAMES)

    @pl.loop(0, 7)
    def _(index):
        rows = pl.ds(pl.multiple_of(index * (ROWS // 7), 16), ROWS // 7)
        own[0, rows, :] = (powers[rows, :] - mean).astype(BF16)


def search_kernel(
    beams,
    volt_hbm,
    taps_ref,
    table_hbm,
    delays_hbm,
    assign_ref,
    widths_ref,
    series_ref,
    snr_ref,
    volt,
    table,
    split,
    delays,
    lookups,
    frames,
    powers,
    slabs,
    total,
    outbox,
    inbox,
    prefix,
    best,
    snr_out,
    plane_sem,
    volt_sem,
    load_sem,
    ring_send,
    ring_recv,
    block_send,
    block_recv,
    local_sem,
):
    me = lax.axis_index("beam")
    sub = lax.axis_index("sub")
    subs = COARSE
    left, right = lax.rem(sub + subs - 1, subs), lax.rem(sub + 1, subs)

    volt_copies = []
    for half in range(2):
        rows = pl.ds(half * (volt.shape[0] // 2), volt.shape[0] // 2)
        copy = pltpu.make_async_copy(volt_hbm.at[rows], volt.at[rows], volt_sem.at[half])
        copy.start()
        volt_copies.append((copy, rows))
    table_copy = pltpu.make_async_copy(table_hbm, table, load_sem.at[0])
    table_copy.start()

    barrier = pltpu.get_barrier_semaphore()
    for side in (left, right):
        pl.semaphore_signal(barrier, inc=1, device_id={"sub": side}, device_id_type=MESH)

    line = 8
    planes = beams // line
    plane, place = lax.div(me, line), lax.rem(me, line)
    others_of_place = [
        lax.rem(plane + hop, planes) * line + place for hop in range(1, planes)
    ]
    others_of_plane = [
        plane * line + lax.rem(place + hop, line) for hop in range(1, line)
    ]
    hops = [(0, 0), (0, 1), (0, 3), (1, 0), (3, 0), (0, 2), (2, 0), (1, 1)]
    hops += [(3, 3), (1, 3), (3, 1), (1, 2), (2, 1), (3, 2), (2, 3), (2, 2)]
    hops = [hop for hop in reversed(hops) if hop[0] < planes]
    others = [
        lax.rem(plane + far, planes) * line
        + lax.rem(place + 2 * near, line)
        + (core if core == 0 else 1 - 2 * lax.rem(place, 2))
        for far, near in hops
        for core in range(2)
        if (far, near, core) != (0, 0, 0)
    ]
    for peer in others_of_place + others_of_plane:
        pl.semaphore_signal(barrier, inc=1, device_id={"beam": peer}, device_id_type=MESH)

    delays_copy = pltpu.make_async_copy(
        delays_hbm.at[:, pl.ds(pl.multiple_of(sub * 16, 16), 16), :], delays, load_sem.at[1]
    )
    channelize(
        volt_hbm,
        taps_ref,
        volt,
        volt_copies,
        table,
        split,
        table_copy,
        delays_copy.start,
        frames,
        powers,
        slabs,
    )
    pl.semaphore_wait(barrier, 2 + planes - 1 + line - 1)
    for peer in others_of_place:
        pl.semaphore_signal(plane_sem, inc=1, device_id={"beam": peer}, device_id_type=MESH)

    def ring(source, target, first, count, side, which):
        return pltpu.make_async_remote_copy(
            src_ref=slabs.at[source, pl.ds(first, count)],
            dst_ref=slabs.at[target, pl.ds(first, count)],
            send_sem=ring_send.at[which],
            recv_sem=ring_recv.at[which],
            device_id={"sub": side},
            device_id_type=MESH,
        )

    near, far = [], []
    for piece, (first, count) in enumerate(CUTS):
        near.append(
            (
                ring(0, 1, first, count, right, 4 * piece),
                ring(0, 2, first, count, left, 4 * piece + 1),
            )
        )
        half = 128
        far.append(
            (
                ring(1, 3, first, half, right, 4 * piece + 2),
                ring(2, 3, first + half, count - half, left, 4 * piece + 3),
            )
        )

    def pass_on(piece):
        for arrived, onward in zip(near[piece], far[piece]):
            arrived.wait_recv()
            onward.start()

    for copy in near[0]:
        copy.start()
    delays_copy.wait()

    @pl.loop(0, beams)
    def _(owner):
        rows = pl.ds(pl.multiple_of(owner * 16, 16), 16)
        for slot, hop in enumerate((0, subs - 1, 1, 2)):
            coarse = lax.rem(sub + hop, subs)
            lanes = pl.ds(pl.multiple_of(coarse * FINE, FINE), FINE)
            lookup = delays[assign_ref[me, owner], :, lanes]
            lookups[slot, rows, :] = lookup.astype(F32).astype(BF16)

    def product(slots, start, count):
        onehots, shifts = [], []
        for slot in slots:
            window = slabs[slot, pl.ds(start, count + SHIFTS), :]
            lookup = lookups[slot]
            for shift in range(SHIFTS):
                shifts.append(window[shift : shift + count])
                onehots.append(jnp.where(lookup == BF16(shift), BF16(1), BF16(0)))
        return lax.dot_general(
            jnp.concatenate(onehots, axis=1),
            jnp.concatenate(shifts, axis=1),
            (((1,), (1,)), ((), ())),
            preferred_element_type=F32,
        )

    scale = 1.0 / math.sqrt(COARSE * FINE)

    def columns(piece):
        return pl.ds(pl.multiple_of(piece * PIECE, PIECE), PIECE)

    def block_copy(piece, owner):
        return pltpu.make_async_remote_copy(
            src_ref=outbox.at[piece, owner],
            dst_ref=inbox.at[piece, me],
            send_sem=block_send.at[piece],
            recv_sem=block_recv.at[piece],
            device_id={"beam": owner},
            device_id_type=MESH,
        )

    def out_copy(piece):
        return pltpu.make_async_copy(
            inbox.at[piece], series_ref.at[0, :, :, columns(piece)], local_sem.at[piece]
        )

    def deliver(piece):
        series = (total[piece] * scale).astype(BF16)
        outbox[piece] = series.reshape(beams, 16, PIECE)
        for owner in others:
            block_copy(piece, owner).start()
        inbox[piece, pl.ds(me, 1)] = outbox[piece, pl.ds(me, 1)]

    def add_prefix(piece, series):
        count = PIECE + MAXW + 16
        triangle = jnp.where(
            lax.broadcasted_iota(jnp.int32, (count, PIECE), 1)
            < lax.broadcasted_iota(jnp.int32, (count, PIECE), 0),
            1.0,
            0.0,
        ).astype(BF16)
        sums = lax.dot_general(
            triangle, series, (((1,), (1,)), ((), ())), preferred_element_type=F32
        )
        start = pl.multiple_of(piece * PIECE, PIECE)
        for tile in range(lane_tiles):
            carry = prefix[tile, pl.ds(start, 8), :][0:1]
            prefix[tile, pl.ds(start, count), :] = (
                sums[:, tile * 128 : (tile + 1) * 128] + carry
            )

    lane_tiles = beams * 16 // 128
    prefix[:, 0:8, :] = jnp.zeros((lane_tiles, 8, 128), F32)
    best[...] = jnp.full(best.shape, -jnp.inf, F32)
    widths = [widths_ref[box] for box in range(NBOX)]
    for copy in near[1]:
        copy.start()
    @pl.loop(0, PIECES)
    def _(piece):
        @pl.when(piece == 2)
        def _():
            pass_on(0)
            for copy in near[2]:
                copy.start()

        total[piece] = product((0,), pl.multiple_of(piece * PIECE, PIECE), PIECE)


    @pl.loop(0, PIECES)
    def _(piece):
        start = pl.multiple_of(piece * PIECE, PIECE)
        @pl.loop(1, 3)
        def _(slot):
            total[piece] += product((slot,), start, PIECE)


        for later in range(1, PIECES):

            @pl.when(piece == later - 1)
            def _():
                pass_on(later)

        @pl.when(piece == 0)
        def _():
            pl.semaphore_wait(plane_sem, planes - 1)

        for now in range(PIECES):

            @pl.when(piece == now)
            def _():
                for copy in far[now]:
                    copy.wait_recv()

        total[piece] += product((3,), start, PIECE)

        deliver(piece)

    @pl.loop(0, PIECES)
    def _(piece):
        all_blocks = pltpu.make_async_remote_copy(
            src_ref=outbox.at[piece, pl.ds(0, beams - 1)],
            dst_ref=inbox.at[piece, pl.ds(0, beams - 1)],
            send_sem=block_send.at[piece],
            recv_sem=block_recv.at[piece],
            device_id={"beam": me},
            device_id_type=MESH,
        )
        all_blocks.wait_recv()
        out_copy(piece).start()
        add_prefix(piece, inbox[piece].reshape(beams * 16, PIECE))
        first = jnp.where(piece == 0, 0, piece * PIECE - MAXW)
        stop = jnp.where(piece == PIECES - 1, TOUT, (piece + 1) * PIECE - MAXW)
        boxcars(widths, prefix, best, first, stop)
        all_blocks.wait_send()

    finish_boxcars(widths, best, snr_out)
    snr_ref[...] = jnp.transpose(snr_out[:, :, 0:16], (2, 1, 0))
    for piece in range(PIECES):
        out_copy(piece).wait()
    for piece in range(PIECES):
        for copy in near[piece] + far[piece]:
            copy.wait_send()


def boxcars(widths, prefix, best, first, stop):
    block = MAXW

    @pl.loop(0, prefix.shape[0])
    def _(tile):
        def step(index, tops):
            start = pl.multiple_of(first + index * block, block)
            base = prefix[tile, pl.ds(start, block), :]
            out = []
            for box in range(NBOX):
                gain = prefix[tile, pl.ds(start + widths[box], block), :] - base
                top = jnp.max(gain.reshape(block // 8, 8, 128), axis=0)
                out.append(jnp.maximum(tops[box], top))
            return tuple(out)

        tops = tuple(best[tile, box] for box in range(NBOX))
        tops = lax.fori_loop(0, (stop - first) // block, step, tops)
        for box in range(NBOX):
            best[tile, box] = tops[box]


def finish_boxcars(widths, best, snr_out):
    root = [
        1.0 / jnp.sqrt(jnp.full((1, 128), width, jnp.int32).astype(F32)) for width in widths
    ]

    @pl.loop(0, best.shape[0])
    def _(tile):
        rows = [
            jnp.max(best[tile, box], axis=0, keepdims=True) * root[box] for box in range(NBOX)
        ]
        rows = jnp.concatenate(rows, axis=0)
        for owner in range(8):
            snr_out[tile * 8 + owner] = pltpu.roll(rows, (128 - 16 * owner) % 128, 1)


def hand_over(chunks, series_from, snr_from, series_to, snr_to, series, snr, into, out):
    count = series.shape[1] // chunks
    steps = [(snr_from, snr, snr_to)]
    for chunk in range(chunks):
        rows = pl.ds(chunk * count, count)
        steps.append((series_from.at[:, rows], series.at[:, rows], series_to.at[:, rows]))
    loads = [
        pltpu.make_async_copy(source, held, into.at[index])
        for index, (source, held, target) in enumerate(steps)
    ]
    stores = [
        pltpu.make_async_copy(held, target, out.at[index])
        for index, (source, held, target) in enumerate(steps)
    ]
    for load in loads:
        load.start()
    for load, store in zip(loads, stores):
        load.wait()
        store.start()
    for store in stores:
        store.wait()


def on_device(beams, voltages, pfb_taps, delays, assignment, widths):
    span = delays.shape[0] // beams
    own_span = span // COARSE
    assert own_span == 16
    vmem = pl.BlockSpec(memory_space=pltpu.VMEM)
    smem = pl.BlockSpec(memory_space=pltpu.SMEM)
    anywhere = pl.BlockSpec(memory_space=pl.ANY)
    chans = COARSE * FINE
    rows = beams * own_span
    series, snr = pl.pallas_call(
        functools.partial(search_kernel, beams),
        out_shape=(
            jax.ShapeDtypeStruct((1, beams, own_span, TOUT), BF16),
            jax.ShapeDtypeStruct((own_span, NBOX, beams), F32),
        ),
        in_specs=[anywhere, vmem, anywhere, anywhere, smem, smem],
        out_specs=(anywhere, vmem),
        scratch_shapes=[
            pltpu.VMEM((4 * voltages.shape[-2], 128), BF16),
            pltpu.VMEM((2, FINE, FINE), F32),
            pltpu.VMEM((2, 2 * FINE, 2 * FINE), BF16),
            pltpu.VMEM((beams, own_span, chans), jnp.int32),
            pltpu.VMEM((COARSE, rows, FINE), BF16),
            pltpu.VMEM((4 * (ROWS + 16), 128), F32),
            pltpu.VMEM((ROWS, FINE), F32),
            pltpu.VMEM((COARSE, ROWS, FINE), BF16),
            pltpu.VMEM((PIECES, rows, PIECE), F32),
            pltpu.VMEM((PIECES, beams, own_span, PIECE), BF16),
            pltpu.VMEM((PIECES, beams, own_span, PIECE), BF16),
            pltpu.VMEM((rows // 128, TOUT + MAXW + 16, 128), F32),
            pltpu.VMEM((rows // 128, NBOX, 8, 128), F32),
            pltpu.VMEM((beams, NBOX, 128), F32),
            pltpu.SemaphoreType.REGULAR,
            pltpu.SemaphoreType.DMA((2,)),
            pltpu.SemaphoreType.DMA((2,)),
            pltpu.SemaphoreType.DMA((4 * PIECES,)),
            pltpu.SemaphoreType.DMA((4 * PIECES,)),
            pltpu.SemaphoreType.DMA((PIECES,)),
            pltpu.SemaphoreType.DMA((PIECES,)),
            pltpu.SemaphoreType.DMA((PIECES,)),
        ],
        compiler_params=pltpu.CompilerParams(
            collective_id=0, has_side_effects=True, vmem_limit_bytes=60 << 20
        ),
    )(
        voltages.reshape(2, -1, 2, 128).transpose(1, 2, 0, 3).reshape(-1, 128),
        pfb_taps,
        jnp.asarray(dft_table()),
        delays.reshape(beams, span, chans),
        assignment,
        widths,
    )
    chunks = 8
    series, snr = pl.pallas_call(
        functools.partial(hand_over, chunks),
        out_shape=(
            jax.ShapeDtypeStruct(series.shape, series.dtype),
            jax.ShapeDtypeStruct(snr.shape, snr.dtype),
        ),
        in_specs=[anywhere, anywhere],
        out_specs=(anywhere, anywhere),
        scratch_shapes=[
            pltpu.VMEM(series.shape, series.dtype),
            pltpu.VMEM(snr.shape, snr.dtype),
            pltpu.SemaphoreType.DMA((chunks + 1,)),
            pltpu.SemaphoreType.DMA((chunks + 1,)),
        ],
        compiler_params=pltpu.CompilerParams(vmem_limit_bytes=60 << 20),
    )(series, snr)
    return series, snr.transpose(2, 0, 1)[None]


def solution(mesh):
    in_specs = (P(None, "beam", "sub", None, None), P(), P(), P(), P())
    out_specs = (P("beam", None, "sub", None), P("beam", None, "sub", None))
    return jax.shard_map(
        functools.partial(on_device, mesh.shape["beam"]),
        mesh=mesh,
        in_specs=in_specs,
        out_specs=out_specs,
        check_vma=False,
    )
```

```python
import functools
import math

import jax
import jax.numpy as jnp
import numpy as np
from jax import lax
from jax.experimental import pallas as pl
from jax.experimental.pallas import tpu as pltpu
from jax.sharding import PartitionSpec as P

FINE = 256
COARSE = 4
TAPS = 16
SHIFTS = 16
NBOX = 8
MAXW = 32
TOUT = 768
FRAMES = TOUT + SHIFTS - 1
ROWS = 784
PIECE = 256
PIECES = TOUT // PIECE
CUTS = ((0, 272), (272, 256), (528, 256))
BLOCK = 784
MESH = pl.DeviceIdType.MESH
BF16 = jnp.bfloat16
F32 = jnp.float32


def dft_table():
    position = np.arange(FINE)
    angles = (position[:, None] * position[None, :] % FINE) * (2.0 * math.pi / FINE)
    return (np.stack([np.cos(angles), np.sin(angles)]) / math.sqrt(FINE)).astype(np.float32)


def channelize(
    volt_hbm, taps_ref, volt, volt_copies, table, split, table_copy, start_late, frames, powers, own
):
    count = volt_hbm.shape[0]
    frames[count:, :] = jnp.zeros((frames.shape[0] - count, 128), F32)
    for copy, rows in volt_copies:
        copy.wait()
        frames[rows, :] = volt[rows, :].astype(F32)
    table_copy.wait()
    for index in range(2):
        exact = table[index]
        high = exact.astype(BF16)
        low = (exact - high.astype(F32)).astype(BF16)
        for which, value in enumerate((high, low)):
            if index == 0:
                split[which, 0:FINE, 0:FINE] = value
                split[which, FINE:, FINE:] = value
            else:
                split[which, 0:FINE, FINE:] = -value
                split[which, FINE:, 0:FINE] = value
    start_late()
    taps = taps_ref[...]

    def step(index, total):
        start = pl.multiple_of(index * BLOCK, 8)
        halves = []
        for part in range(2):
            for side in range(2):
                weights = taps[:, side * 128 : (side + 1) * 128]
                value = 0.0
                for tap in range(TAPS):
                    first = 4 * (start + tap) + 2 * side + part
                    value = value + weights[tap : tap + 1] * frames[
                        pl.ds(first, BLOCK, stride=4), :
                    ]
                halves.append(value)
        stacked = jnp.concatenate(halves, axis=1)
        high = stacked.astype(BF16)
        low = (stacked - high.astype(F32)).astype(BF16)
        spectra = (
            jnp.dot(high, split[0], preferred_element_type=F32)
            + jnp.dot(low, split[0], preferred_element_type=F32)
            + jnp.dot(high, split[1], preferred_element_type=F32)
        )
        power = spectra[:, :FINE] ** 2 + spectra[:, FINE:] ** 2
        frame = start + lax.broadcasted_iota(jnp.int32, (BLOCK, FINE), 0)
        power = jnp.where(frame < FRAMES, power, 0.0)
        powers[pl.ds(start, BLOCK), :] = power
        return total + jnp.sum(power, axis=0, keepdims=True)

    total = lax.fori_loop(0, ROWS // BLOCK, step, jnp.zeros((1, FINE), F32))
    mean = total * (1.0 / FRAMES)

    @pl.loop(0, 7)
    def _(index):
        rows = pl.ds(pl.multiple_of(index * (ROWS // 7), 16), ROWS // 7)
        own[0, rows, :] = (powers[rows, :] - mean).astype(BF16)


def search_kernel(
    beams,
    volt_hbm,
    taps_ref,
    table_hbm,
    delays_hbm,
    assign_ref,
    widths_ref,
    series_ref,
    snr_ref,
    volt,
    table,
    split,
    delays,
    lookups,
    frames,
    powers,
    slabs,
    total,
    outbox,
    inbox,
    prefix,
    best,
    snr_out,
    plane_sem,
    volt_sem,
    load_sem,
    ring_send,
    ring_recv,
    block_send,
    block_recv,
    local_sem,
):
    me = lax.axis_index("beam")
    sub = lax.axis_index("sub")
    subs = COARSE
    left, right = lax.rem(sub + subs - 1, subs), lax.rem(sub + 1, subs)

    volt_copies = []
    for half in range(2):
        rows = pl.ds(half * (volt.shape[0] // 2), volt.shape[0] // 2)
        copy = pltpu.make_async_copy(volt_hbm.at[rows], volt.at[rows], volt_sem.at[half])
        copy.start()
        volt_copies.append((copy, rows))
    table_copy = pltpu.make_async_copy(table_hbm, table, load_sem.at[0])
    table_copy.start()

    barrier = pltpu.get_barrier_semaphore()
    for side in (left, right):
        pl.semaphore_signal(barrier, inc=1, device_id={"sub": side}, device_id_type=MESH)

    line = 8
    planes = beams // line
    plane, place = lax.div(me, line), lax.rem(me, line)
    others_of_place = [
        lax.rem(plane + hop, planes) * line + place for hop in range(1, planes)
    ]
    others_of_plane = [
        plane * line + lax.rem(place + hop, line) for hop in range(1, line)
    ]
    hops = [(0, 0), (0, 1), (0, 3), (1, 0), (3, 0), (0, 2), (2, 0), (1, 1)]
    hops += [(3, 3), (1, 3), (3, 1), (1, 2), (2, 1), (3, 2), (2, 3), (2, 2)]
    hops = [hop for hop in reversed(hops) if hop[0] < planes]
    others = [
        lax.rem(plane + far, planes) * line
        + lax.rem(place + 2 * near, line)
        + (core if core == 0 else 1 - 2 * lax.rem(place, 2))
        for far, near in hops
        for core in range(2)
        if (far, near, core) != (0, 0, 0)
    ]
    for peer in others_of_place + others_of_plane:
        pl.semaphore_signal(barrier, inc=1, device_id={"beam": peer}, device_id_type=MESH)

    delays_copy = pltpu.make_async_copy(
        delays_hbm.at[:, pl.ds(pl.multiple_of(sub * 16, 16), 16), :], delays, load_sem.at[1]
    )
    channelize(
        volt_hbm,
        taps_ref,
        volt,
        volt_copies,
        table,
        split,
        table_copy,
        delays_copy.start,
        frames,
        powers,
        slabs,
    )
    pl.semaphore_wait(barrier, 2 + planes - 1 + line - 1)
    for peer in others_of_place:
        pl.semaphore_signal(plane_sem, inc=1, device_id={"beam": peer}, device_id_type=MESH)

    def ring(source, target, first, count, side, which):
        return pltpu.make_async_remote_copy(
            src_ref=slabs.at[source, pl.ds(first, count)],
            dst_ref=slabs.at[target, pl.ds(first, count)],
            send_sem=ring_send.at[which],
            recv_sem=ring_recv.at[which],
            device_id={"sub": side},
            device_id_type=MESH,
        )

    near, far = [], []
    for piece, (first, count) in enumerate(CUTS):
        near.append(
            (
                ring(0, 1, first, count, right, 4 * piece),
                ring(0, 2, first, count, left, 4 * piece + 1),
            )
        )
        half = 128
        far.append(
            (
                ring(1, 3, first, half, right, 4 * piece + 2),
                ring(2, 3, first + half, count - half, left, 4 * piece + 3),
            )
        )

    def pass_on(piece):
        for arrived, onward in zip(near[piece], far[piece]):
            arrived.wait_recv()
            onward.start()

    for copy in near[0]:
        copy.start()
    delays_copy.wait()

    @pl.loop(0, beams)
    def _(owner):
        rows = pl.ds(pl.multiple_of(owner * 16, 16), 16)
        for slot, hop in enumerate((0, subs - 1, 1, 2)):
            coarse = lax.rem(sub + hop, subs)
            lanes = pl.ds(pl.multiple_of(coarse * FINE, FINE), FINE)
            lookup = delays[assign_ref[me, owner], :, lanes]
            lookups[slot, rows, :] = lookup.astype(F32).astype(BF16)

    def product(slots, start, count):
        onehots, shifts = [], []
        for slot in slots:
            window = slabs[slot, pl.ds(start, count + SHIFTS), :]
            lookup = lookups[slot]
            for shift in range(SHIFTS):
                shifts.append(window[shift : shift + count])
                onehots.append(jnp.where(lookup == BF16(shift), BF16(1), BF16(0)))
        return lax.dot_general(
            jnp.concatenate(onehots, axis=1),
            jnp.concatenate(shifts, axis=1),
            (((1,), (1,)), ((), ())),
            preferred_element_type=F32,
        )

    scale = 1.0 / math.sqrt(COARSE * FINE)

    def columns(piece):
        return pl.ds(pl.multiple_of(piece * PIECE, PIECE), PIECE)

    def block_copy(piece, owner):
        return pltpu.make_async_remote_copy(
            src_ref=outbox.at[piece, owner],
            dst_ref=inbox.at[piece, me],
            send_sem=block_send.at[piece],
            recv_sem=block_recv.at[piece],
            device_id={"beam": owner},
            device_id_type=MESH,
        )

    def out_copy(piece):
        return pltpu.make_async_copy(
            inbox.at[piece], series_ref.at[0, :, :, columns(piece)], local_sem.at[piece]
        )

    def deliver(piece):
        series = (total[piece] * scale).astype(BF16)
        outbox[piece] = series.reshape(beams, 16, PIECE)
        for owner in others:
            block_copy(piece, owner).start()
        inbox[piece, pl.ds(me, 1)] = outbox[piece, pl.ds(me, 1)]

    def add_prefix(piece, series):
        count = PIECE + MAXW + 16
        triangle = jnp.where(
            lax.broadcasted_iota(jnp.int32, (count, PIECE), 1)
            < lax.broadcasted_iota(jnp.int32, (count, PIECE), 0),
            1.0,
            0.0,
        ).astype(BF16)
        sums = lax.dot_general(
            triangle, series, (((1,), (1,)), ((), ())), preferred_element_type=F32
        )
        start = pl.multiple_of(piece * PIECE, PIECE)
        for tile in range(lane_tiles):
            carry = prefix[tile, pl.ds(start, 8), :][0:1]
            prefix[tile, pl.ds(start, count), :] = (
                sums[:, tile * 128 : (tile + 1) * 128] + carry
            )

    lane_tiles = beams * 16 // 128
    prefix[:, 0:8, :] = jnp.zeros((lane_tiles, 8, 128), F32)
    best[...] = jnp.full(best.shape, -jnp.inf, F32)
    widths = [widths_ref[box] for box in range(NBOX)]
    for copy in near[1]:
        copy.start()
    @pl.loop(0, PIECES)
    def _(piece):
        @pl.when(piece == 2)
        def _():
            pass_on(0)
            for copy in near[2]:
                copy.start()

        total[piece] = product((0,), pl.multiple_of(piece * PIECE, PIECE), PIECE)


    @pl.loop(0, PIECES)
    def _(piece):
        start = pl.multiple_of(piece * PIECE, PIECE)
        @pl.loop(1, 3)
        def _(slot):
            total[piece] += product((slot,), start, PIECE)


        for later in range(1, PIECES):

            @pl.when(piece == later - 1)
            def _():
                pass_on(later)

        @pl.when(piece == 0)
        def _():
            pl.semaphore_wait(plane_sem, planes - 1)

        for now in range(PIECES):

            @pl.when(piece == now)
            def _():
                for copy in far[now]:
                    copy.wait_recv()

        total[piece] += product((3,), start, PIECE)

        deliver(piece)

    @pl.loop(0, PIECES)
    def _(piece):
        all_blocks = pltpu.make_async_remote_copy(
            src_ref=outbox.at[piece, pl.ds(0, beams - 1)],
            dst_ref=inbox.at[piece, pl.ds(0, beams - 1)],
            send_sem=block_send.at[piece],
            recv_sem=block_recv.at[piece],
            device_id={"beam": me},
            device_id_type=MESH,
        )
        all_blocks.wait_recv()
        out_copy(piece).start()
        add_prefix(piece, inbox[piece].reshape(beams * 16, PIECE))
        first = jnp.where(piece == 0, 0, piece * PIECE - MAXW)
        stop = jnp.where(piece == PIECES - 1, TOUT, (piece + 1) * PIECE - MAXW)
        boxcars(widths, prefix, best, first, stop)
        all_blocks.wait_send()

    finish_boxcars(widths, best, snr_out)
    snr_ref[...] = jnp.transpose(snr_out[:, :, 0:16], (2, 1, 0))
    for piece in range(PIECES):
        out_copy(piece).wait()
    for piece in range(PIECES):
        for copy in near[piece] + far[piece]:
            copy.wait_send()


def boxcars(widths, prefix, best, first, stop):
    block = MAXW

    @pl.loop(0, prefix.shape[0])
    def _(tile):
        def step(index, tops):
            start = pl.multiple_of(first + index * block, block)
            base = prefix[tile, pl.ds(start, block), :]
            out = []
            for box in range(NBOX):
                gain = prefix[tile, pl.ds(start + widths[box], block), :] - base
                top = jnp.max(gain.reshape(block // 8, 8, 128), axis=0)
                out.append(jnp.maximum(tops[box], top))
            return tuple(out)

        tops = tuple(best[tile, box] for box in range(NBOX))
        tops = lax.fori_loop(0, (stop - first) // block, step, tops)
        for box in range(NBOX):
            best[tile, box] = tops[box]


def finish_boxcars(widths, best, snr_out):
    root = [
        1.0 / jnp.sqrt(jnp.full((1, 128), width, jnp.int32).astype(F32)) for width in widths
    ]

    @pl.loop(0, best.shape[0])
    def _(tile):
        rows = [
            jnp.max(best[tile, box], axis=0, keepdims=True) * root[box] for box in range(NBOX)
        ]
        rows = jnp.concatenate(rows, axis=0)
        for owner in range(8):
            snr_out[tile * 8 + owner] = pltpu.roll(rows, (128 - 16 * owner) % 128, 1)


def hand_over(chunks, series_from, snr_from, series_to, snr_to, series, snr, into, out):
    count = series.shape[1] // chunks
    steps = [(snr_from, snr, snr_to)]
    for chunk in range(chunks):
        rows = pl.ds(chunk * count, count)
        steps.append((series_from.at[:, rows], series.at[:, rows], series_to.at[:, rows]))
    loads = [
        pltpu.make_async_copy(source, held, into.at[index])
        for index, (source, held, target) in enumerate(steps)
    ]
    stores = [
        pltpu.make_async_copy(held, target, out.at[index])
        for index, (source, held, target) in enumerate(steps)
    ]
    for load in loads:
        load.start()
    for load, store in zip(loads, stores):
        load.wait()
        store.start()
    for store in stores:
        store.wait()


def on_device(beams, voltages, pfb_taps, delays, assignment, widths):
    span = delays.shape[0] // beams
    own_span = span // COARSE
    assert own_span == 16
    vmem = pl.BlockSpec(memory_space=pltpu.VMEM)
    smem = pl.BlockSpec(memory_space=pltpu.SMEM)
    anywhere = pl.BlockSpec(memory_space=pl.ANY)
    chans = COARSE * FINE
    rows = beams * own_span
    series, snr = pl.pallas_call(
        functools.partial(search_kernel, beams),
        out_shape=(
            jax.ShapeDtypeStruct((1, beams, own_span, TOUT), BF16),
            jax.ShapeDtypeStruct((own_span, NBOX, beams), F32),
        ),
        in_specs=[anywhere, vmem, anywhere, anywhere, smem, smem],
        out_specs=(anywhere, vmem),
        scratch_shapes=[
            pltpu.VMEM((4 * voltages.shape[-2], 128), BF16),
            pltpu.VMEM((2, FINE, FINE), F32),
            pltpu.VMEM((2, 2 * FINE, 2 * FINE), BF16),
            pltpu.VMEM((beams, own_span, chans), jnp.int32),
            pltpu.VMEM((COARSE, rows, FINE), BF16),
            pltpu.VMEM((4 * (ROWS + 16), 128), F32),
            pltpu.VMEM((ROWS, FINE), F32),
            pltpu.VMEM((COARSE, ROWS, FINE), BF16),
            pltpu.VMEM((PIECES, rows, PIECE), F32),
            pltpu.VMEM((PIECES, beams, own_span, PIECE), BF16),
            pltpu.VMEM((PIECES, beams, own_span, PIECE), BF16),
            pltpu.VMEM((rows // 128, TOUT + MAXW + 16, 128), F32),
            pltpu.VMEM((rows // 128, NBOX, 8, 128), F32),
            pltpu.VMEM((beams, NBOX, 128), F32),
            pltpu.SemaphoreType.REGULAR,
            pltpu.SemaphoreType.DMA((2,)),
            pltpu.SemaphoreType.DMA((2,)),
            pltpu.SemaphoreType.DMA((4 * PIECES,)),
            pltpu.SemaphoreType.DMA((4 * PIECES,)),
            pltpu.SemaphoreType.DMA((PIECES,)),
            pltpu.SemaphoreType.DMA((PIECES,)),
            pltpu.SemaphoreType.DMA((PIECES,)),
        ],
        compiler_params=pltpu.CompilerParams(
            collective_id=0, has_side_effects=True, vmem_limit_bytes=60 << 20
        ),
    )(
        voltages.reshape(2, -1, 2, 128).transpose(1, 2, 0, 3).reshape(-1, 128),
        pfb_taps,
        jnp.asarray(dft_table()),
        delays.reshape(beams, span, chans),
        assignment,
        widths,
    )
    chunks = 8
    series, snr = pl.pallas_call(
        functools.partial(hand_over, chunks),
        out_shape=(
            jax.ShapeDtypeStruct(series.shape, series.dtype),
            jax.ShapeDtypeStruct(snr.shape, snr.dtype),
        ),
        in_specs=[anywhere, anywhere],
        out_specs=(anywhere, anywhere),
        scratch_shapes=[
            pltpu.VMEM(series.shape, series.dtype),
            pltpu.VMEM(snr.shape, snr.dtype),
            pltpu.SemaphoreType.DMA((chunks + 1,)),
            pltpu.SemaphoreType.DMA((chunks + 1,)),
        ],
        compiler_params=pltpu.CompilerParams(vmem_limit_bytes=60 << 20),
    )(series, snr)
    return series, snr.transpose(2, 0, 1)[None]


def solution(mesh):
    in_specs = (P(None, "beam", "sub", None, None), P(), P(), P(), P())
    out_specs = (P("beam", None, "sub", None), P("beam", None, "sub", None))
    return jax.shard_map(
        functools.partial(on_device, mesh.shape["beam"]),
        mesh=mesh,
        in_specs=in_specs,
        out_specs=out_specs,
        check_vma=False,
    )
```

```python
import functools
import math

import jax
import jax.numpy as jnp
import numpy as np
from jax import lax
from jax.experimental import pallas as pl
from jax.experimental.pallas import tpu as pltpu
from jax.sharding import PartitionSpec as P

FINE = 256
COARSE = 4
TAPS = 16
SHIFTS = 16
NBOX = 8
MAXW = 32
TOUT = 768
FRAMES = TOUT + SHIFTS - 1
ROWS = 784
PIECE = 256
PIECES = TOUT // PIECE
CUTS = ((0, 272), (272, 256), (528, 256))
BLOCK = 784
MESH = pl.DeviceIdType.MESH
BF16 = jnp.bfloat16
F32 = jnp.float32


def dft_table():
    position = np.arange(FINE)
    angles = (position[:, None] * position[None, :] % FINE) * (2.0 * math.pi / FINE)
    return (np.stack([np.cos(angles), np.sin(angles)]) / math.sqrt(FINE)).astype(np.float32)


def channelize(
    volt_hbm, taps_ref, volt, volt_copies, table, split, table_copy, frames, powers, own
):
    count = volt_hbm.shape[0]
    frames[count:, :] = jnp.zeros((frames.shape[0] - count, 128), F32)
    for copy, rows in volt_copies:
        copy.wait()
        frames[rows, :] = volt[rows, :].astype(F32)
    table_copy.wait()
    for index in range(2):
        exact = table[index]
        high = exact.astype(BF16)
        low = (exact - high.astype(F32)).astype(BF16)
        for which, value in enumerate((high, low)):
            if index == 0:
                split[which, 0:FINE, 0:FINE] = value
                split[which, FINE:, FINE:] = value
            else:
                split[which, 0:FINE, FINE:] = -value
                split[which, FINE:, 0:FINE] = value
    taps = taps_ref[...]

    def step(index, total):
        start = pl.multiple_of(index * BLOCK, 8)
        halves = []
        for part in range(2):
            for side in range(2):
                weights = taps[:, side * 128 : (side + 1) * 128]
                value = 0.0
                for tap in range(TAPS):
                    first = 4 * (start + tap) + 2 * side + part
                    value = value + weights[tap : tap + 1] * frames[
                        pl.ds(first, BLOCK, stride=4), :
                    ]
                halves.append(value)
        stacked = jnp.concatenate(halves, axis=1)
        high = stacked.astype(BF16)
        low = (stacked - high.astype(F32)).astype(BF16)
        spectra = (
            jnp.dot(high, split[0], preferred_element_type=F32)
            + jnp.dot(low, split[0], preferred_element_type=F32)
            + jnp.dot(high, split[1], preferred_element_type=F32)
        )
        power = spectra[:, :FINE] ** 2 + spectra[:, FINE:] ** 2
        frame = start + lax.broadcasted_iota(jnp.int32, (BLOCK, FINE), 0)
        power = jnp.where(frame < FRAMES, power, 0.0)
        powers[pl.ds(start, BLOCK), :] = power
        return total + jnp.sum(power, axis=0, keepdims=True)

    total = lax.fori_loop(0, ROWS // BLOCK, step, jnp.zeros((1, FINE), F32))
    mean = total * (1.0 / FRAMES)

    @pl.loop(0, 7)
    def _(index):
        rows = pl.ds(pl.multiple_of(index * (ROWS // 7), 16), ROWS // 7)
        own[0, rows, :] = (powers[rows, :] - mean).astype(BF16)


def search_kernel(
    beams,
    volt_hbm,
    taps_ref,
    table_hbm,
    delays_hbm,
    assign_ref,
    widths_ref,
    series_ref,
    snr_ref,
    volt,
    table,
    split,
    delays,
    lookups,
    frames,
    powers,
    slabs,
    total,
    outbox,
    inbox,
    prefix,
    best,
    snr_out,
    plane_sem,
    volt_sem,
    load_sem,
    ring_send,
    ring_recv,
    block_send,
    block_recv,
    local_sem,
):
    me = lax.axis_index("beam")
    sub = lax.axis_index("sub")
    subs = COARSE
    left, right = lax.rem(sub + subs - 1, subs), lax.rem(sub + 1, subs)

    volt_copies = []
    for half in range(2):
        rows = pl.ds(half * (volt.shape[0] // 2), volt.shape[0] // 2)
        copy = pltpu.make_async_copy(volt_hbm.at[rows], volt.at[rows], volt_sem.at[half])
        copy.start()
        volt_copies.append((copy, rows))
    table_copy = pltpu.make_async_copy(table_hbm, table, load_sem.at[0])
    table_copy.start()

    barrier = pltpu.get_barrier_semaphore()
    for side in (left, right):
        pl.semaphore_signal(barrier, inc=1, device_id={"sub": side}, device_id_type=MESH)

    line = 8
    planes = beams // line
    plane, place = lax.div(me, line), lax.rem(me, line)
    others_of_place = [
        lax.rem(plane + hop, planes) * line + place for hop in range(1, planes)
    ]
    others_of_plane = [
        plane * line + lax.rem(place + hop, line) for hop in range(1, line)
    ]
    hops = [(0, 0), (0, 1), (0, 3), (1, 0), (3, 0), (0, 2), (2, 0), (1, 1)]
    hops += [(3, 3), (1, 3), (3, 1), (1, 2), (2, 1), (3, 2), (2, 3), (2, 2)]
    hops = [hop for hop in reversed(hops) if hop[0] < planes]
    others = [
        lax.rem(plane + far, planes) * line
        + lax.rem(place + 2 * near, line)
        + (core if core == 0 else 1 - 2 * lax.rem(place, 2))
        for far, near in hops
        for core in range(2)
        if (far, near, core) != (0, 0, 0)
    ]
    for peer in others_of_place + others_of_plane:
        pl.semaphore_signal(barrier, inc=1, device_id={"beam": peer}, device_id_type=MESH)

    delays_copy = pltpu.make_async_copy(
        delays_hbm.at[:, pl.ds(pl.multiple_of(sub * 16, 16), 16), :], delays, load_sem.at[1]
    )
    delays_copy.start()
    channelize(
        volt_hbm,
        taps_ref,
        volt,
        volt_copies,
        table,
        split,
        table_copy,
        frames,
        powers,
        slabs,
    )
    pl.semaphore_wait(barrier, 2 + planes - 1 + line - 1)
    for peer in others_of_place:
        pl.semaphore_signal(plane_sem, inc=1, device_id={"beam": peer}, device_id_type=MESH)

    def ring(source, target, first, count, side, which):
        return pltpu.make_async_remote_copy(
            src_ref=slabs.at[source, pl.ds(first, count)],
            dst_ref=slabs.at[target, pl.ds(first, count)],
            send_sem=ring_send.at[which],
            recv_sem=ring_recv.at[which],
            device_id={"sub": side},
            device_id_type=MESH,
        )

    near, far = [], []
    for piece, (first, count) in enumerate(CUTS):
        near.append(
            (
                ring(0, 1, first, count, right, 4 * piece),
                ring(0, 2, first, count, left, 4 * piece + 1),
            )
        )
        half = 128
        far.append(
            (
                ring(1, 3, first, half, right, 4 * piece + 2),
                ring(2, 3, first + half, count - half, left, 4 * piece + 3),
            )
        )

    def pass_on(piece):
        for arrived, onward in zip(near[piece], far[piece]):
            arrived.wait_recv()
            onward.start()

    for copy in near[0]:
        copy.start()
    delays_copy.wait()

    @pl.loop(0, beams)
    def _(owner):
        rows = pl.ds(pl.multiple_of(owner * 16, 16), 16)
        for slot, hop in enumerate((0, subs - 1, 1, 2)):
            coarse = lax.rem(sub + hop, subs)
            lanes = pl.ds(pl.multiple_of(coarse * FINE, FINE), FINE)
            lookup = delays[assign_ref[me, owner], :, lanes]
            lookups[slot, rows, :] = lookup.astype(F32).astype(BF16)

    def product(slots, start, count):
        onehots, shifts = [], []
        for slot in slots:
            window = slabs[slot, pl.ds(start, count + SHIFTS), :]
            lookup = lookups[slot]
            for shift in range(SHIFTS):
                shifts.append(window[shift : shift + count])
                onehots.append(jnp.where(lookup == BF16(shift), BF16(1), BF16(0)))
        return lax.dot_general(
            jnp.concatenate(onehots, axis=1),
            jnp.concatenate(shifts, axis=1),
            (((1,), (1,)), ((), ())),
            preferred_element_type=F32,
        )

    scale = 1.0 / math.sqrt(COARSE * FINE)

    def columns(piece):
        return pl.ds(pl.multiple_of(piece * PIECE, PIECE), PIECE)

    def block_copy(piece, owner):
        return pltpu.make_async_remote_copy(
            src_ref=outbox.at[piece, owner],
            dst_ref=inbox.at[piece, me],
            send_sem=block_send.at[piece],
            recv_sem=block_recv.at[piece],
            device_id={"beam": owner},
            device_id_type=MESH,
        )

    def out_copy(piece):
        return pltpu.make_async_copy(
            inbox.at[piece], series_ref.at[0, :, :, columns(piece)], local_sem.at[piece]
        )

    def deliver(piece):
        series = (total[piece] * scale).astype(BF16)
        outbox[piece] = series.reshape(beams, 16, PIECE)
        for owner in others:
            block_copy(piece, owner).start()
        inbox[piece, pl.ds(me, 1)] = outbox[piece, pl.ds(me, 1)]

    def add_prefix(piece, series):
        count = PIECE + MAXW + 16
        triangle = jnp.where(
            lax.broadcasted_iota(jnp.int32, (count, PIECE), 1)
            < lax.broadcasted_iota(jnp.int32, (count, PIECE), 0),
            1.0,
            0.0,
        ).astype(BF16)
        sums = lax.dot_general(
            triangle, series, (((1,), (1,)), ((), ())), preferred_element_type=F32
        )
        start = pl.multiple_of(piece * PIECE, PIECE)
        for tile in range(lane_tiles):
            carry = prefix[tile, pl.ds(start, 8), :][0:1]
            prefix[tile, pl.ds(start, count), :] = (
                sums[:, tile * 128 : (tile + 1) * 128] + carry
            )

    lane_tiles = beams * 16 // 128
    prefix[:, 0:8, :] = jnp.zeros((lane_tiles, 8, 128), F32)
    best[...] = jnp.full(best.shape, -jnp.inf, F32)
    widths = [widths_ref[box] for box in range(NBOX)]
    for copy in near[1]:
        copy.start()
    @pl.loop(0, PIECES)
    def _(piece):
        @pl.when(piece == 2)
        def _():
            pass_on(0)
            for copy in near[2]:
                copy.start()

        total[piece] = product((0,), pl.multiple_of(piece * PIECE, PIECE), PIECE)


    @pl.loop(0, PIECES)
    def _(piece):
        start = pl.multiple_of(piece * PIECE, PIECE)
        @pl.loop(1, 3)
        def _(slot):
            total[piece] += product((slot,), start, PIECE)


        for later in range(1, PIECES):

            @pl.when(piece == later - 1)
            def _():
                pass_on(later)

        @pl.when(piece == 0)
        def _():
            pl.semaphore_wait(plane_sem, planes - 1)

        for now in range(PIECES):

            @pl.when(piece == now)
            def _():
                for copy in far[now]:
                    copy.wait_recv()

        total[piece] += product((3,), start, PIECE)

        deliver(piece)

    @pl.loop(0, PIECES)
    def _(piece):
        all_blocks = pltpu.make_async_remote_copy(
            src_ref=outbox.at[piece, pl.ds(0, beams - 1)],
            dst_ref=inbox.at[piece, pl.ds(0, beams - 1)],
            send_sem=block_send.at[piece],
            recv_sem=block_recv.at[piece],
            device_id={"beam": me},
            device_id_type=MESH,
        )
        all_blocks.wait_recv()
        out_copy(piece).start()
        add_prefix(piece, inbox[piece].reshape(beams * 16, PIECE))
        first = jnp.where(piece == 0, 0, piece * PIECE - MAXW)
        stop = jnp.where(piece == PIECES - 1, TOUT, (piece + 1) * PIECE - MAXW)
        boxcars(widths, prefix, best, first, stop)
        all_blocks.wait_send()

    finish_boxcars(widths, best, snr_out)
    snr_ref[...] = jnp.transpose(snr_out[:, :, 0:16], (2, 1, 0))
    for piece in range(PIECES):
        out_copy(piece).wait()
    for piece in range(PIECES):
        for copy in near[piece] + far[piece]:
            copy.wait_send()


def boxcars(widths, prefix, best, first, stop):
    block = MAXW

    @pl.loop(0, prefix.shape[0])
    def _(tile):
        def step(index, tops):
            start = pl.multiple_of(first + index * block, block)
            base = prefix[tile, pl.ds(start, block), :]
            out = []
            for box in range(NBOX):
                gain = prefix[tile, pl.ds(start + widths[box], block), :] - base
                top = jnp.max(gain.reshape(block // 8, 8, 128), axis=0)
                out.append(jnp.maximum(tops[box], top))
            return tuple(out)

        tops = tuple(best[tile, box] for box in range(NBOX))
        tops = lax.fori_loop(0, (stop - first) // block, step, tops)
        for box in range(NBOX):
            best[tile, box] = tops[box]


def finish_boxcars(widths, best, snr_out):
    root = [
        1.0 / jnp.sqrt(jnp.full((1, 128), width, jnp.int32).astype(F32)) for width in widths
    ]

    @pl.loop(0, best.shape[0])
    def _(tile):
        rows = [
            jnp.max(best[tile, box], axis=0, keepdims=True) * root[box] for box in range(NBOX)
        ]
        rows = jnp.concatenate(rows, axis=0)
        for owner in range(8):
            snr_out[tile * 8 + owner] = pltpu.roll(rows, (128 - 16 * owner) % 128, 1)


def hand_over(chunks, series_from, snr_from, series_to, snr_to, series, snr, into, out):
    count = series.shape[1] // chunks
    steps = [(snr_from, snr, snr_to)]
    for chunk in range(chunks):
        rows = pl.ds(chunk * count, count)
        steps.append((series_from.at[:, rows], series.at[:, rows], series_to.at[:, rows]))
    loads = [
        pltpu.make_async_copy(source, held, into.at[index])
        for index, (source, held, target) in enumerate(steps)
    ]
    stores = [
        pltpu.make_async_copy(held, target, out.at[index])
        for index, (source, held, target) in enumerate(steps)
    ]
    for load in loads:
        load.start()
    for load, store in zip(loads, stores):
        load.wait()
        store.start()
    for store in stores:
        store.wait()


def on_device(beams, voltages, pfb_taps, delays, assignment, widths):
    span = delays.shape[0] // beams
    own_span = span // COARSE
    assert own_span == 16
    vmem = pl.BlockSpec(memory_space=pltpu.VMEM)
    smem = pl.BlockSpec(memory_space=pltpu.SMEM)
    anywhere = pl.BlockSpec(memory_space=pl.ANY)
    chans = COARSE * FINE
    rows = beams * own_span
    series, snr = pl.pallas_call(
        functools.partial(search_kernel, beams),
        out_shape=(
            jax.ShapeDtypeStruct((1, beams, own_span, TOUT), BF16),
            jax.ShapeDtypeStruct((own_span, NBOX, beams), F32),
        ),
        in_specs=[anywhere, vmem, anywhere, anywhere, smem, smem],
        out_specs=(anywhere, vmem),
        scratch_shapes=[
            pltpu.VMEM((4 * voltages.shape[-2], 128), BF16),
            pltpu.VMEM((2, FINE, FINE), F32),
            pltpu.VMEM((2, 2 * FINE, 2 * FINE), BF16),
            pltpu.VMEM((beams, own_span, chans), jnp.int32),
            pltpu.VMEM((COARSE, rows, FINE), BF16),
            pltpu.VMEM((4 * (ROWS + 16), 128), F32),
            pltpu.VMEM((ROWS, FINE), F32),
            pltpu.VMEM((COARSE, ROWS, FINE), BF16),
            pltpu.VMEM((PIECES, rows, PIECE), F32),
            pltpu.VMEM((PIECES, beams, own_span, PIECE), BF16),
            pltpu.VMEM((PIECES, beams, own_span, PIECE), BF16),
            pltpu.VMEM((rows // 128, TOUT + MAXW + 16, 128), F32),
            pltpu.VMEM((rows // 128, NBOX, 8, 128), F32),
            pltpu.VMEM((beams, NBOX, 128), F32),
            pltpu.SemaphoreType.REGULAR,
            pltpu.SemaphoreType.DMA((2,)),
            pltpu.SemaphoreType.DMA((2,)),
            pltpu.SemaphoreType.DMA((4 * PIECES,)),
            pltpu.SemaphoreType.DMA((4 * PIECES,)),
            pltpu.SemaphoreType.DMA((PIECES,)),
            pltpu.SemaphoreType.DMA((PIECES,)),
            pltpu.SemaphoreType.DMA((PIECES,)),
        ],
        compiler_params=pltpu.CompilerParams(
            collective_id=0, has_side_effects=True, vmem_limit_bytes=60 << 20
        ),
    )(
        voltages.reshape(2, -1, 2, 128).transpose(1, 2, 0, 3).reshape(-1, 128),
        pfb_taps,
        jnp.asarray(dft_table()),
        delays.reshape(beams, span, chans),
        assignment,
        widths,
    )
    chunks = 8
    series, snr = pl.pallas_call(
        functools.partial(hand_over, chunks),
        out_shape=(
            jax.ShapeDtypeStruct(series.shape, series.dtype),
            jax.ShapeDtypeStruct(snr.shape, snr.dtype),
        ),
        in_specs=[anywhere, anywhere],
        out_specs=(anywhere, anywhere),
        scratch_shapes=[
            pltpu.VMEM(series.shape, series.dtype),
            pltpu.VMEM(snr.shape, snr.dtype),
            pltpu.SemaphoreType.DMA((chunks + 1,)),
            pltpu.SemaphoreType.DMA((chunks + 1,)),
        ],
        compiler_params=pltpu.CompilerParams(vmem_limit_bytes=60 << 20),
    )(series, snr)
    return series, snr.transpose(2, 0, 1)[None]


def solution(mesh):
    in_specs = (P(None, "beam", "sub", None, None), P(), P(), P(), P())
    out_specs = (P("beam", None, "sub", None), P("beam", None, "sub", None))
    return jax.shard_map(
        functools.partial(on_device, mesh.shape["beam"]),
        mesh=mesh,
        in_specs=in_specs,
        out_specs=out_specs,
        check_vma=False,
    )
```
